512 devices in a mesh: dom: 128 (over y, z, core), sub: 4 (over x).
Axes of the slice: x: 4, y: 8, z: 8, core: 2. Of those that a mesh axis runs over, the one named last changes fastest.
Arguments:
- features: bfloat16 [262144, 128], P(('dom', 'sub')), may hold values from -32 to 32
- cotangent: bfloat16 [262144, 128], P(('dom', 'sub')), may hold values from -13 to 13
- w_query: bfloat16 [128, 128], replicated, may hold values from -0.5 to 0.5
- w_key: bfloat16 [128, 128], replicated, may hold values from -0.5 to 0.5
- w_value: bfloat16 [128, 128], replicated, may hold values from -0.5 to 0.5
- w_graph: bfloat16 [128, 128], replicated, may hold values from -0.5 to 0.5
- send_rows: int32 [512, 512, 4], P(('dom', 'sub')), may hold values from -1 to 511, as said below
- block_col: int32 [512, 4, 4], P(('dom', 'sub')), may hold values from 0 to 19
- block_count: int32 [512, 4], P(('dom', 'sub')), may hold values from 1 to 4, as said below
- block_vals: bfloat16 [512, 4, 4, 128, 128], P(('dom', 'sub')), may hold values from -0.25 to 0.25
Outputs:
- grad_features: bfloat16 [262144, 128], P(('dom', 'sub'))
- grad_query: float32 [128, 128], replicated
- grad_key: float32 [128, 128], replicated
- grad_value: float32 [128, 128], replicated
- grad_graph: float32 [128, 128], replicated
The draws below stay inside these ranges and needn't reach their ends.
Inputs may be any that keep to these rules, and one draw needn't show every extreme that they name: send_rows[p, q, s] is the row, among partition p's 512 rows, placed in slot s of what partition p sends to partition q, or -1 for an empty slot; the live slots of a pair come first, every pair has one or more, and in every draw some pairs fill all 4 slots and some leave slots empty. `block_count`: each partition's first row block has its largest count, and partition 0 reaches 4.
All inputs are finite; a program needn't handle non-finite values.
Results may differ from the reference program's by a relative error of at most 0.0015.
Values may be sent and summed in bfloat16 or wider, within the bound.
A program may use at most 64 MiB of HBM per device.

```python
import math
import jax
import jax.numpy as jnp
from jax import lax

D = 128
ROWS = 512
SLOTS = 4
BLK = 128
NB = 4
PARTS_SIZE = 512
NODES = 262144
RB = 4
EXTB = 20


def shaped_rows(key, noise, common_weight, part_weight, low_scale, top_scale, part_low, part_span):
    key_common, key_part, key_scale = jax.random.split(key, 3)
    common = jnp.clip(jax.random.normal(key_common, (D,), jnp.float32), -3.0, 3.0)
    part_mean = jnp.clip(jax.random.normal(key_part, (PARTS_SIZE, D), jnp.float32), -3.0, 3.0)
    steps_along = jnp.arange(PARTS_SIZE, dtype=jnp.float32) / (PARTS_SIZE - 1)
    part_level = part_low * jnp.exp(part_span * steps_along)
    row_scale = jnp.exp(jax.random.uniform(key_scale, (NODES, 1), jnp.float32, math.log(low_scale), math.log(top_scale)))
    mixed = noise + common_weight * common[None, :] + part_weight * jnp.repeat(part_mean, ROWS, axis=0)
    return row_scale * jnp.repeat(part_level, ROWS)[:, None] * mixed


def draw_features(key, part):
    key = jax.random.fold_in(key, 11)
    key_noise, key_rest = jax.random.split(key)
    noise = jnp.clip(jax.random.normal(key_noise, (NODES, D), jnp.float32), -4.0, 4.0)
    return shaped_rows(key_rest, noise, 0.5, 0.4, 0.5, 2.0, 0.6, math.log(3.0)).astype(jnp.bfloat16)


def draw_cotangent(key, part):
    key = jax.random.fold_in(key, 12)
    key_noise, key_rest = jax.random.split(key)
    noise = jnp.clip(jax.random.normal(key_noise, (NODES, D), jnp.float32), -4.0, 4.0)
    return shaped_rows(key_rest, noise, 0.3, 0.3, 0.5, 2.0, 0.3, math.log(3.0)).astype(jnp.bfloat16)


def draw_send_rows(key, part):
    key = jax.random.fold_in(key, 13)
    key_count, key_rows = jax.random.split(key)
    order = jnp.arange(PARTS_SIZE, dtype=jnp.int32)
    following = order[None, :] == (order[:, None] + 1) % PARTS_SIZE
    itself = order[None, :] == order[:, None]
    counts = jax.random.randint(key_count, (PARTS_SIZE, PARTS_SIZE), 1, SLOTS + 1, dtype=jnp.int32)
    counts = jnp.where(itself, 1, jnp.where(following, SLOTS, counts))
    picks = jax.random.randint(key_rows, (PARTS_SIZE, PARTS_SIZE, SLOTS), 0, ROWS, dtype=jnp.int32)
    slot_ids = jnp.arange(SLOTS, dtype=jnp.int32)
    picks = jnp.where(following[:, :, None] & (slot_ids == 0)[None, None, :], ROWS - 1, picks)
    return jnp.where(slot_ids[None, None, :] < counts[:, :, None], picks, -1).astype(jnp.int32)


def draw_block_count(key, part):
    key = jax.random.fold_in(key, 14)
    key_level, key_count = jax.random.split(key)
    level = jax.random.randint(key_level, (PARTS_SIZE,), 1, NB + 1, dtype=jnp.int32)
    level = level.at[0].set(NB)
    counts = jax.random.randint(key_count, (PARTS_SIZE, RB), 1, NB + 1, dtype=jnp.int32)
    counts = jnp.minimum(counts, level[:, None])
    counts = counts.at[:, 0].set(level)
    return counts.astype(jnp.int32)


def touch_ends(entries, own_key, least, high):
    longest = entries.shape.index(max(entries.shape))
    spots = []
    for shift in (0, 1):
        where = [jax.random.randint(jax.random.fold_in(own_key, axis), (), 0, length) for axis, length in enumerate(entries.shape)]
        where[longest] = (where[longest] + shift) % entries.shape[longest]
        spots.append(tuple(where))
    return entries.at[spots[0]].set(least).at[spots[1]].set(high)


def steps_of(rng, extent, pieces, least, top_value):
    level = 1.0
    for axis_at, blocks in pieces:
        draws = jax.random.uniform(jax.random.fold_in(jax.random.fold_in(rng, 6), axis_at), (blocks,), jnp.float32, least / len(pieces), top_value / len(pieces))
        level = level * jnp.repeat(jnp.exp(draws), extent[axis_at] // blocks).reshape((-1,) + (1,) * (len(extent) - 1 - axis_at))
    return level


def scatter_about(key, extent, deviation, bound, cuts=(), kind=jnp.bfloat16):
    result = jax.random.normal(key, extent, jnp.float32) * deviation
    if len(cuts) > 0:
        result = steps_of(key, extent, cuts, -0.22, 0.18) * result
    return jnp.clip(result, min=-bound, max=bound).astype(kind)


def setup_inputs(seed: int = 0) -> dict:
    key_list = jax.random.split(jax.random.key(seed), 11)
    return {
        "features": draw_features(jax.random.fold_in(key_list[10], 71), 0),
        "cotangent": draw_cotangent(jax.random.fold_in(key_list[10], 71), 0),
        "w_query": scatter_about(key_list[2], (D, D), D ** -0.5, 0.5),
        "w_key": scatter_about(key_list[3], (D, D), D ** -0.5, 0.5),
        "w_value": scatter_about(key_list[4], (D, D), D ** -0.5, 0.5),
        "w_graph": scatter_about(key_list[5], (D, D), D ** -0.5, 0.5),
        "send_rows": draw_send_rows(jax.random.fold_in(key_list[10], 71), 0),
        "block_col": touch_ends(jax.random.randint(key_list[7], (PARTS_SIZE, RB, NB), 0, EXTB), jax.random.fold_in(key_list[7], 1), 0, EXTB - 1).astype(jnp.int32),
        "block_count": draw_block_count(jax.random.fold_in(key_list[10], 71), 0),
        "block_vals": scatter_about(key_list[9], (PARTS_SIZE, RB, NB, BLK, BLK), (BLK * NB) ** -0.5, 0.25, ((0, 512),)),
    }


def feature_map(inner):
    return jnp.where(inner > 0, inner + 1.0, jnp.exp(jnp.minimum(inner, 0.0)))


def map_slope(inner):
    return jnp.where(inner > 0, jnp.ones_like(inner), jnp.exp(jnp.minimum(inner, 0.0)))


def project(rows_in, w_query, w_key, w_value):
    queries = jnp.dot(rows_in, w_query, preferred_element_type=jnp.float32)
    key_rows = jnp.dot(rows_in, w_key, preferred_element_type=jnp.float32)
    value_rows = jnp.dot(rows_in, w_value, preferred_element_type=jnp.float32)
    return queries, key_rows, value_rows


def reference(features, cotangent, w_query, w_key, w_value, w_graph, send_rows, block_col, block_count, block_vals):
    highest = lax.Precision.HIGHEST
    state_scale = 1.0 / (NODES * D)
    feat_parts = features.reshape(PARTS_SIZE, ROWS, D)
    cot_parts = cotangent.reshape(PARTS_SIZE, ROWS, D)

    def state_step(running, feat_part):
        queries, key_rows, value_rows = project(feat_part, w_query, w_key, w_value)
        mapped_keys = feature_map(key_rows)
        return (running[0] + jnp.dot(mapped_keys.T, value_rows, precision=highest),
                running[1] + jnp.sum(mapped_keys, axis=0)), None

    (value_state, key_sum), unused = lax.scan(
        state_step, (jnp.zeros((D, D), jnp.float32), jnp.zeros((D,), jnp.float32)), feat_parts)

    def attention_terms(feat_part, cot_part):
        queries, key_rows, value_rows = project(feat_part, w_query, w_key, w_value)
        mapped_queries = feature_map(queries)
        mapped_keys = feature_map(key_rows)
        denominator = 1.0 + state_scale * jnp.dot(mapped_queries, key_sum, precision=highest)
        attended = (state_scale * jnp.dot(mapped_queries, value_state, precision=highest) + value_rows) / denominator[:, None]
        cot_wide = cot_part.astype(jnp.float32)
        grad_num = cot_wide / denominator[:, None]
        grad_den = -jnp.sum(cot_wide * attended, axis=1) / denominator
        return queries, key_rows, value_rows, mapped_queries, mapped_keys, grad_num, grad_den

    def grad_step(running, inputs):
        feat_part, cot_part = inputs
        outcome = attention_terms(feat_part, cot_part)
        mapped_queries, grad_num, grad_den = outcome[3], outcome[5], outcome[6]
        return (running[0] + state_scale * jnp.dot(mapped_queries.T, grad_num, precision=highest),
                running[1] + state_scale * jnp.dot(grad_den, mapped_queries, precision=highest)), None

    (grad_state, grad_ksum), unused = lax.scan(
        grad_step, (jnp.zeros((D, D), jnp.float32), jnp.zeros((D,), jnp.float32)), (feat_parts, cot_parts))

    part_ids = jnp.arange(PARTS_SIZE, dtype=jnp.int32)
    block_ids = jnp.arange(NB, dtype=jnp.int32)
    source_base = part_ids[:, None] * ROWS

    def graph_step(running, inputs):
        grad_graph, grad_gcn = running
        part_index, cot_part, incoming, column_ids, counts, weights = inputs
        slot_live = incoming >= 0
        global_rows = (source_base + jnp.maximum(incoming, 0)).reshape(-1)
        halo_rows = jnp.where(slot_live.reshape(-1)[:, None], features[global_rows], jnp.zeros((), features.dtype))
        own_rows = lax.dynamic_slice_in_dim(features, part_index * ROWS, ROWS, 0)
        extended = jnp.concatenate([own_rows, halo_rows], axis=0).reshape(EXTB, BLK, D)
        block_live = block_ids[None, :] < counts[:, None]
        masked = jnp.where(block_live[:, :, None, None], weights, jnp.zeros((), weights.dtype)).astype(jnp.float32)
        picked = extended[column_ids].astype(jnp.float32)
        aggregated = jnp.einsum("rnij,rnjd->rid", masked, picked, precision=highest).reshape(ROWS, D)
        grad_graph = grad_graph + jnp.dot(aggregated.T, cot_part.astype(jnp.float32), precision=highest)
        graph_in = jnp.dot(cot_part, w_graph.T, preferred_element_type=jnp.float32)
        contrib = jnp.einsum("rnij,rid->rnjd", masked, graph_in.reshape(RB, BLK, D), precision=highest)
        ext_grad = jax.ops.segment_sum(contrib.reshape(RB * NB, BLK, D), column_ids.reshape(-1),
                                       num_segments=EXTB).reshape(EXTB * BLK, D)
        own_old = lax.dynamic_slice_in_dim(grad_gcn, part_index * ROWS, ROWS, 0)
        grad_gcn = lax.dynamic_update_slice_in_dim(grad_gcn, own_old + ext_grad[:ROWS], part_index * ROWS, 0)
        drop_rows = jnp.where(slot_live, source_base + incoming, NODES).reshape(-1)
        grad_gcn = grad_gcn.at[drop_rows].add(ext_grad[ROWS:], mode="drop")
        return (grad_graph, grad_gcn), None

    (grad_graph, grad_gcn), unused = lax.scan(
        graph_step,
        (jnp.zeros((D, D), jnp.float32), jnp.zeros((NODES, D), jnp.float32)),
        (part_ids, cot_parts, jnp.transpose(send_rows, (1, 0, 2)), block_col, block_count, block_vals))

    wide_query = w_query.astype(jnp.float32)
    wide_key = w_key.astype(jnp.float32)
    wide_value = w_value.astype(jnp.float32)

    def final_step(running, inputs):
        feat_part, cot_part, gcn_part = inputs
        queries, key_rows, value_rows, mapped_queries, mapped_keys, grad_num, grad_den = attention_terms(feat_part, cot_part)
        grad_mapq = state_scale * (jnp.dot(grad_num, value_state.T, precision=highest) + grad_den[:, None] * key_sum[None, :])
        grad_mapk = jnp.dot(value_rows, grad_state.T, precision=highest) + grad_ksum[None, :]
        grad_values = grad_num + jnp.dot(mapped_keys, grad_state, precision=highest)
        grad_queries = grad_mapq * map_slope(queries)
        grad_keys = grad_mapk * map_slope(key_rows)
        grad_in = (jnp.dot(grad_queries, wide_query.T, precision=highest)
                   + jnp.dot(grad_keys, wide_key.T, precision=highest)
                   + jnp.dot(grad_values, wide_value.T, precision=highest) + gcn_part)
        wide_feat = feat_part.astype(jnp.float32)
        running = (running[0] + jnp.dot(wide_feat.T, grad_queries, precision=highest),
                   running[1] + jnp.dot(wide_feat.T, grad_keys, precision=highest),
                   running[2] + jnp.dot(wide_feat.T, grad_values, precision=highest))
        return running, grad_in.astype(jnp.bfloat16)

    zero_square = jnp.zeros((D, D), jnp.float32)
    (grad_query, grad_key, grad_value), grad_rows = lax.scan(
        final_step, (zero_square, zero_square, zero_square),
        (feat_parts, cot_parts, grad_gcn.reshape(PARTS_SIZE, ROWS, D)))
    grad_features = grad_rows.reshape(NODES, D)
    return (grad_features, grad_query / NODES, grad_key / NODES, grad_value / NODES, grad_graph / NODES)
```

```python
import functools

import jax
import jax.numpy as jnp
from jax import lax
from jax.experimental import pallas as pl
from jax.experimental.pallas import tpu as pltpu
from jax.sharding import PartitionSpec as P

highest = lax.Precision.HIGHEST
MESH = pl.DeviceIdType.MESH


def place():
    dom = lax.axis_index("dom")
    return dom // 16, (dom // 2) % 8, dom % 2, lax.axis_index("sub")


def plane_member(index):
    row, col, core, along = place()
    return ((row * 8 + index // 4) * 2 + core, index % 4)


def column_member(index):
    row, col, core, along = place()
    return (index // 2 * 16 + col * 2 + index % 2, along)


def each_other(count, me, act):
    def body(step, carry):
        act((me + step) % count)
        return carry

    lax.fori_loop(1, count, body, 0)


def sum_kernel(in_ref, out_ref, got_a, part, got_b, whole, send_sem, recv_sem):
    row, col, core, along = place()
    mine_a, mine_b = col * 4 + along, row * 2 + core
    barrier = pltpu.get_barrier_semaphore()

    def greet(member):
        def act(index):
            pl.semaphore_signal(barrier, inc=1, device_id=member(index), device_id_type=MESH)

        return act

    def push(member, source, target, phase):
        def act(index):
            pltpu.make_async_remote_copy(
                src_ref=source(index),
                dst_ref=target,
                send_sem=send_sem.at[phase],
                recv_sem=recv_sem.at[phase],
                device_id=member(index),
                device_id_type=MESH,
            ).start()

        return act

    def drain(ref, sem):
        pltpu.make_async_copy(ref, ref, sem).wait()

    each_other(32, mine_a, greet(plane_member))
    each_other(16, mine_b, greet(column_member))
    pl.semaphore_wait(barrier, 46)
    each_other(32, mine_a, push(plane_member, lambda index: in_ref.at[index], got_a.at[mine_a], 0))
    got_a[mine_a] = in_ref[mine_a]
    drain(got_a.at[pl.ds(0, 31)], recv_sem.at[0])
    part[...] = jnp.sum(got_a[...], axis=0)
    each_other(16, mine_b, push(column_member, lambda index: part, got_b.at[mine_b], 1))
    got_b[mine_b] = part[...]
    drain(got_b.at[pl.ds(0, 15)], recv_sem.at[1])
    total = jnp.sum(got_b[...], axis=0)
    whole[...] = total
    each_other(32, mine_a, push(plane_member, lambda index: whole, out_ref.at[mine_a], 2))
    out_ref[mine_a] = total
    drain(got_a.at[pl.ds(0, 31)], recv_sem.at[2])
    drain(got_a.at[pl.ds(0, 31)], send_sem.at[0])
    drain(got_b.at[pl.ds(0, 15)], send_sem.at[1])
    drain(got_a.at[pl.ds(0, 31)], send_sem.at[2])


def all_sum(values, collective_id):
    rows = values.shape[1]
    vmem = pl.BlockSpec(memory_space=pltpu.VMEM)
    return pl.pallas_call(
        sum_kernel,
        out_shape=jax.ShapeDtypeStruct(values.shape, jnp.float32),
        in_specs=[vmem],
        out_specs=vmem,
        scratch_shapes=[
            pltpu.VMEM((32, rows, 128), jnp.float32),
            pltpu.VMEM((rows, 128), jnp.float32),
            pltpu.VMEM((16, rows, 128), jnp.float32),
            pltpu.VMEM((rows, 128), jnp.float32),
            pltpu.SemaphoreType.DMA((3,)),
            pltpu.SemaphoreType.DMA((3,)),
        ],
        compiler_params=pltpu.CompilerParams(collective_id=collective_id, has_side_effects=True),
        name="all_sum_%d" % rows,
    )(values)


def sum_square_and_row(square, row, collective_id):
    extra = jnp.zeros((32, 1, 128), jnp.float32).at[0, 0].set(row)
    out = all_sum(jnp.concatenate([square.reshape(32, 4, 128), extra], axis=1), collective_id)
    return out[:, :4].reshape(128, 128), out[0, 4]


def sum_squares(squares, collective_id):
    stacked = jnp.concatenate([square.reshape(32, 4, 128) for square in squares], axis=1)
    out = all_sum(stacked, collective_id)
    return [out[:, 4 * at : 4 * at + 4].reshape(128, 128) for at in range(len(squares))]


def feature_map(inner):
    return jnp.where(inner > 0, inner + 1.0, jnp.exp(jnp.minimum(inner, 0.0)))


def map_slope(inner):
    return jnp.where(inner > 0, jnp.ones_like(inner), jnp.exp(jnp.minimum(inner, 0.0)))


def shards(
    features,
    cotangent,
    w_query,
    w_key,
    w_value,
    w_graph,
    send_rows,
    block_col,
    block_count,
    block_vals,
):
    rows_here, feat_width = features.shape
    dom_count = lax.axis_size("dom")
    sub_count = lax.axis_size("sub")
    part_count = dom_count * sub_count
    block_size = block_vals.shape[-1]
    per_block = block_col.shape[-1]
    row_blocks = block_col.shape[1]
    slot_count = send_rows.shape[-1]
    node_count = rows_here * part_count
    state_scale = 1.0 / (node_count * feat_width)
    ext_blocks = (rows_here + part_count * slot_count) // block_size
    targets = send_rows[0]
    slot_live = targets >= 0
    column_ids = block_col[0]
    block_live = jnp.arange(per_block, dtype=jnp.int32)[None, :] < block_count[0][:, None]
    masked = jnp.where(block_live[:, :, None, None], block_vals[0], jnp.zeros((), block_vals.dtype))
    onehot = (
        column_ids.reshape(-1)[:, None] == jnp.arange(ext_blocks, dtype=jnp.int32)[None, :]
    ).astype(jnp.float32)
    taken = jnp.take(features, jnp.maximum(targets, 0).reshape(-1), axis=0)
    outgoing = jnp.where(slot_live.reshape(-1)[:, None], taken, jnp.zeros((), features.dtype))
    outgoing = outgoing.reshape(dom_count, sub_count, slot_count, feat_width)
    arrived = lax.all_to_all(
        lax.all_to_all(outgoing, "dom", split_axis=0, concat_axis=0, tiled=True),
        "sub",
        split_axis=1,
        concat_axis=1,
        tiled=True,
    )
    extended = jnp.concatenate([features, arrived.reshape(-1, feat_width)], axis=0)
    picked = extended.reshape(ext_blocks, block_size, feat_width)[column_ids]
    aggregated = jnp.einsum(
        "rnij,rnjd->rid", masked, picked, preferred_element_type=jnp.float32
    ).reshape(rows_here, feat_width)
    graph_part = jnp.dot(
        aggregated.T, cotangent, precision=highest, preferred_element_type=jnp.float32
    )
    graph_in = jnp.dot(cotangent, w_graph.T, preferred_element_type=jnp.float32)
    right_blocks = graph_in.reshape(row_blocks, block_size, feat_width)
    contrib = jnp.einsum(
        "rnij,rid->rnjd",
        masked,
        right_blocks,
        precision=highest,
        preferred_element_type=jnp.float32,
    )
    summed = jnp.einsum(
        "ke,kx->ex",
        onehot,
        contrib.reshape(row_blocks * per_block, block_size * feat_width),
        precision=highest,
    )
    ext_grad = summed.reshape(ext_blocks * block_size, feat_width)
    own_part = ext_grad[:rows_here]
    boundary = ext_grad[rows_here:].reshape(dom_count, sub_count, slot_count, feat_width)
    returned = lax.all_to_all(
        lax.all_to_all(boundary, "dom", split_axis=0, concat_axis=0, tiled=True),
        "sub",
        split_axis=1,
        concat_axis=1,
        tiled=True,
    )
    drop_index = jnp.where(slot_live, targets, rows_here).reshape(-1)
    grad_gcn = own_part.at[drop_index].add(returned.reshape(-1, feat_width), mode="drop")
    graph_part = graph_part / node_count
    queries = jnp.dot(features, w_query, preferred_element_type=jnp.float32)
    key_rows = jnp.dot(features, w_key, preferred_element_type=jnp.float32)
    value_rows = jnp.dot(features, w_value, preferred_element_type=jnp.float32)
    mapped_queries = feature_map(queries)
    mapped_keys = feature_map(key_rows)
    value_state, key_sum = sum_square_and_row(
        jnp.dot(mapped_keys.T, value_rows, precision=highest), jnp.sum(mapped_keys, axis=0), 0
    )
    denominator = 1.0 + state_scale * jnp.dot(mapped_queries, key_sum, precision=highest)
    attended = (
        state_scale * jnp.dot(mapped_queries, value_state, precision=highest) + value_rows
    ) / denominator[:, None]
    cot_wide = cotangent.astype(jnp.float32)
    grad_num = cot_wide / denominator[:, None]
    grad_den = -jnp.sum(cot_wide * attended, axis=1) / denominator
    state_part = state_scale * jnp.dot(mapped_queries.T, grad_num, precision=highest)
    ksum_part = state_scale * jnp.dot(grad_den, mapped_queries, precision=highest)
    grad_state, grad_ksum = sum_square_and_row(state_part, ksum_part, 1)
    grad_mapq = state_scale * (
        jnp.dot(grad_num, value_state.T, precision=highest) + grad_den[:, None] * key_sum[None, :]
    )
    grad_mapk = jnp.dot(value_rows, grad_state.T, precision=highest) + grad_ksum[None, :]
    grad_values = grad_num + jnp.dot(mapped_keys, grad_state, precision=highest)
    grad_queries = grad_mapq * map_slope(queries)
    grad_keys = grad_mapk * map_slope(key_rows)
    grad_in = (
        jnp.dot(grad_queries, w_query.T, precision=highest, preferred_element_type=jnp.float32)
        + jnp.dot(grad_keys, w_key.T, precision=highest, preferred_element_type=jnp.float32)
        + jnp.dot(grad_values, w_value.T, precision=highest, preferred_element_type=jnp.float32)
        + grad_gcn
    )
    grad_features = grad_in.astype(jnp.bfloat16)
    query_part = (
        jnp.dot(features.T, grad_queries, precision=highest, preferred_element_type=jnp.float32)
        / node_count
    )
    key_part = (
        jnp.dot(features.T, grad_keys, precision=highest, preferred_element_type=jnp.float32)
        / node_count
    )
    value_part = (
        jnp.dot(features.T, grad_values, precision=highest, preferred_element_type=jnp.float32)
        / node_count
    )
    grad_query, grad_key, grad_value, grad_graph = sum_squares(
        (query_part, key_part, value_part, graph_part), 2
    )
    return (grad_features, grad_query, grad_key, grad_value, grad_graph)


def solution(mesh):
    return jax.shard_map(
        shards,
        mesh=mesh,
        in_specs=(
            P(("dom", "sub"), None),
            P(("dom", "sub"), None),
            P(),
            P(),
            P(),
            P(),
            P(("dom", "sub"), None, None),
            P(("dom", "sub"), None, None),
            P(("dom", "sub"), None),
            P(("dom", "sub"), None, None, None, None),
        ),
        out_specs=(P(("dom", "sub"), None), P(), P(), P(), P()),
        check_vma=False,
    )
```

```python
import jax
import jax.numpy as jnp
from jax import lax
from jax.experimental import pallas as pl
from jax.experimental.pallas import tpu as pltpu
from jax.sharding import PartitionSpec as P

MESH = pl.DeviceIdType.MESH
F32 = jnp.float32
BF16 = jnp.bfloat16
NODES = 262144
SCALE = 1.0 / (NODES * 128)

KS1, KS2, VS1, VS2, VS3, GS1, GS2, GS3, GK1, GK2 = range(10)
PV1, PV2, PV3, QS1, QS2, QS3, GG1, GG2, GG3 = range(10, 19)
FA, FB, RA, RB = range(19, 23)
EXCHANGES = 23


def place():
    dom = lax.axis_index("dom")
    return dom // 16, (dom // 2) % 8, dom % 2, lax.axis_index("sub")


class Group:
    def __init__(self, count, me, member):
        self.count, self.me, self.member = count, me, member

    def others(self, act):
        def body(step, carry):
            act((self.me + step) % self.count)
            return carry

        lax.fori_loop(1, self.count, body, 0)


def groups():
    y, z, core, x = place()
    plane = Group(32, z * 4 + x, lambda i: ((y * 8 + i // 4) * 2 + core, i % 4))
    column = Group(16, y * 2 + core, lambda i: (i // 2 * 16 + z * 2 + i % 2, x))
    near = Group(8, core * 4 + x, lambda i: ((y * 8 + z) * 2 + i // 4, i % 4))
    far = Group(64, y * 8 + z, lambda i: (i * 2 + core, x))
    return plane, column, near, far


def split(wide):
    high = wide.astype(BF16)
    return high, (wide - high.astype(F32)).astype(BF16)


def dot(left, right, left_dim=1, right_dim=0):
    return lax.dot_general(
        left, right, (((left_dim,), (right_dim,)), ((), ())), preferred_element_type=F32
    )


def dot_wide(left, right, left_dim=1, right_dim=0):
    left_high, left_low = split(left)
    right_high, right_low = split(right)
    return (
        dot(left_high, right_high, left_dim, right_dim)
        + dot(left_high, right_low, left_dim, right_dim)
        + dot(left_low, right_high, left_dim, right_dim)
    )


def dot_exact_left(left, right, left_dim=1, right_dim=0):
    high, low = split(right)
    return dot(left, high, left_dim, right_dim) + dot(left, low, left_dim, right_dim)


def dot_exact_right(left, right, left_dim=1, right_dim=0):
    high, low = split(left)
    return dot(high, right, left_dim, right_dim) + dot(low, right, left_dim, right_dim)


class Sum:
    def __init__(self, src, got, mid, got2, last, whole):
        self.src, self.got, self.mid, self.got2, self.last, self.whole = src, got, mid, got2, last, whole


def sum_buffers(rows, first, second):
    step = rows // first
    return [
        pltpu.VMEM((rows, 128), F32),
        pltpu.VMEM((first, step, 128), F32),
        pltpu.VMEM((step, 128), F32),
        pltpu.VMEM((second, step, 128), F32),
        pltpu.VMEM((step, 128), F32),
        pltpu.VMEM((rows, 128), F32),
    ]


def row_buffers():
    return [
        pltpu.VMEM((1, 128), F32),
        pltpu.VMEM((16, 1, 128), F32),
        pltpu.VMEM((1, 128), F32),
        pltpu.VMEM((32, 1, 128), F32),
        pltpu.VMEM((1, 128), F32),
        pltpu.VMEM((1, 128), F32),
    ]


def layer_kernel(
    feat_ref, cot_ref, wq_ref, wk_ref, wv_ref, wg_ref, rows_ref, col_ref, cols_ref, count_ref, vals_ref,
    out_ref, sums_ref, *scratch
):
    (mk_ref, sk_ref, v_ref, mq_ref, sq_ref, gn_ref, inverse_ref, vg_ref, in_ref) = scratch[:9]
    ks, gk, vs, gs, gg, pv, qs = (Sum(*scratch[9 + 6 * i : 15 + 6 * i]) for i in range(7))
    (onehot, f_out, f_near, f_far, ext, column_rows, contrib, own, b_src, r_out, r_near, r_far, r_got, r_rows,
     send_sem, recv_sem) = scratch[51:]

    plane, column, near, far = groups()
    barrier = pltpu.get_barrier_semaphore()
    for group in (column, plane, near, far):
        group.others(
            lambda i: pl.semaphore_signal(
                barrier, inc=1, device_id=group.member(i), device_id_type=MESH
            )
        )

    pending = []

    def push(group, source, target, which, span):
        def act(i):
            pltpu.make_async_remote_copy(
                src_ref=source(i),
                dst_ref=target,
                send_sem=send_sem.at[which],
                recv_sem=recv_sem.at[which],
                device_id=group.member(i),
                device_id_type=MESH,
            ).start()

        group.others(act)
        pending.append((span, which))

    def wait(span, sem):
        pltpu.make_async_copy(span, span, sem).wait()

    def others_of(ref):
        return ref.at[pl.ds(0, ref.shape[0] - 1)]

    def all_rows(ref, group):
        step = ref.shape[0] // group.count
        return ref.at[pl.ds(0, ref.shape[0] - step)]

    def give(group, source, got, which):
        push(group, source, got.at[group.me], which, others_of(got))

    def take(got, which):
        wait(others_of(got), recv_sem.at[which])
        return jnp.sum(got[...], axis=0)

    def block_of(ref, group, i):
        step = ref.shape[0] // group.count
        return ref.at[pl.ds(pl.multiple_of(i * step, step), step)]

    def scatter(group, src, got, which):
        give(group, lambda i: block_of(src, group, i), got, which)
        got[group.me] = block_of(src, group, group.me)[...]

    def share(group, src, got, which):
        give(group, lambda i: src, got, which)
        got[group.me] = src[...]

    def gather(group, src, whole, which):
        push(group, lambda i: src, block_of(whole, group, group.me), which, all_rows(whole, group))
        block_of(whole, group, group.me)[...] = src[...]

    def feature_map(inner):
        low = jnp.exp(jnp.minimum(inner, 0.0))
        return jnp.where(inner > 0, inner + 1.0, low), jnp.where(inner > 0, 1.0, low)

    feat = feat_ref[...]
    mapped, slope = feature_map(dot(feat, wk_ref[...]))
    mk_ref[...] = mapped
    sk_ref[...] = slope
    ks.src[...] = jnp.sum(mapped, axis=0, keepdims=True)

    pl.semaphore_wait(barrier, 31 + 15 + 7 + 63)
    share(column, ks.src, ks.got, KS1)
    values = dot(feat, wv_ref[...])
    v_ref[...] = values
    vs.src[...] = dot_wide(mapped, values, 0, 0)
    scatter(column, vs.src, vs.got, VS1)

    def mark(at, carry):
        to_near, to_far = at // 8, at % 8
        rows = rows_ref[0, pl.ds(to_far * 64 + to_near, 8, stride=8), :]
        lane = lax.broadcasted_iota(jnp.int32, (8, 512), 1)
        marks = [jnp.where(rows[:, s : s + 1] == lane, 1.0, 0.0) for s in range(4)]
        onehot[to_near, to_far] = jnp.concatenate(marks, axis=0).astype(BF16)
        return carry

    lax.fori_loop(0, 64, mark, 0)

    def pick(at, carry):
        picked = dot(onehot[at].reshape(256, 512), feat_ref[...]).astype(BF16)
        f_out[at] = picked.reshape(8, 32, 128)
        return carry

    lax.fori_loop(0, 8, pick, 0)

    ks.mid[...] = take(ks.got, KS1)
    share(plane, ks.mid, ks.got2, KS2)

    give(near, lambda i: f_out.at[i], f_near, FA)
    f_near[near.me] = f_out[near.me]

    vs.mid[...] = take(vs.got, VS1)
    share(plane, vs.mid, vs.got2, VS2)

    mapped, slope = feature_map(dot(feat_ref[...], wq_ref[...]))
    mq_ref[...] = mapped
    sq_ref[...] = slope

    first = lax.broadcasted_iota(jnp.int32, (256, 256), 0)
    second = lax.broadcasted_iota(jnp.int32, (256, 256), 1)

    def wire_row(natural):
        return ((natural >> 2) & 7) * 32 + (natural & 3) * 8 + (natural >> 5)

    to_natural = jnp.where(second == wire_row(first), 1.0, 0.0).astype(BF16)
    to_wire = jnp.where(first == wire_row(second), 1.0, 0.0).astype(BF16)

    graph_in = dot(cot_ref[...], wg_ref[...], 1, 1)
    for r in range(4):
        right = jnp.concatenate(split(graph_in[r * 128 : (r + 1) * 128]), axis=1)
        for n in range(4):
            term = dot(vals_ref[0, r, n], right, 0, 0)
            contrib[r * 4 + n] = term[:, :128] + term[:, 128:]

    columns = []
    for r in range(4):
        for n in range(4):
            block_at = jnp.broadcast_to(cols_ref[0, r : r + 1, n : n + 1], (1, 128))
            count = jnp.broadcast_to(count_ref[0:1, r : r + 1], (1, 128))
            columns.append(jnp.where(n < count, block_at, -1))
    column_rows[...] = jnp.concatenate(columns, axis=0)

    def column_sum(e):
        chosen = jnp.where(column_rows[...] == e, 1.0, 0.0)
        total = jnp.zeros((128, 128), F32)
        for k in range(16):
            total = total + contrib[k] * chosen[k : k + 1]
        return total

    def own_sum(e, carry):
        own[e] = column_sum(e)
        return carry

    def boundary_sum(e, carry):
        b_src[e] = jnp.concatenate(split(column_sum(e + 4)), axis=1)
        return carry

    lax.fori_loop(0, 4, own_sum, 0)
    lax.fori_loop(0, 16, boundary_sum, 0)

    def order_out(g, carry):
        block = b_src[pl.ds(g * 2, 2)].reshape(256, 256)
        r_out[:, g] = dot(to_wire, block).astype(BF16).reshape(8, 32, 256)
        return carry

    lax.fori_loop(0, 8, order_out, 0)
    give(near, lambda i: r_out.at[i], r_near, RA)
    r_near[near.me] = r_out[near.me]

    key_sum = take(ks.got2, KS2)
    ks.whole[...] = key_sum
    mapped = mq_ref[...]
    inverse = 1.0 / (1.0 + SCALE * jnp.sum(mapped * key_sum, axis=1, keepdims=True))
    inverse_ref[...] = jnp.broadcast_to(inverse, (512, 128))
    grad_num = cot_ref[...].astype(F32) * inverse
    gn_ref[...] = grad_num
    gs.src[...] = SCALE * dot_wide(mapped, grad_num, 0, 0)
    scatter(column, gs.src, gs.got, GS1)

    vs.last[...] = take(vs.got2, VS2)
    gather(column, vs.last, vs.whole, VS3)

    wait(others_of(f_near), recv_sem.at[FA])

    def order_rows(g, carry):
        block = f_near[:, g].reshape(256, 128)
        f_far[pl.ds(g * 8, 8)] = dot(to_natural, block).astype(BF16).reshape(8, 32, 128)
        return carry

    lax.fori_loop(0, 8, order_rows, 0)
    here = ext.at[4 + far.me // 4, pl.ds(pl.multiple_of(far.me % 4 * 32, 32), 32)]
    push(far, lambda i: f_far.at[i], here, FB, others_of(f_far))
    here[...] = f_far[far.me]
    ext[pl.ds(0, 4)] = feat_ref[...].reshape(4, 128, 128)

    gs.mid[...] = take(gs.got, GS1)
    share(plane, gs.mid, gs.got2, GS2)

    wait(all_rows(vs.whole, column), recv_sem.at[VS3])
    value_state = vs.whole[...]
    mapped = mq_ref[...]
    inverse = inverse_ref[...]
    attended = (SCALE * dot_wide(mapped, value_state) + v_ref[...]) * inverse
    grad_den = -jnp.sum(cot_ref[...].astype(F32) * attended, axis=1, keepdims=True) * inverse
    gk.src[...] = SCALE * jnp.sum(grad_den * mapped, axis=0, keepdims=True)
    share(column, gk.src, gk.got, GK1)
    grad_q = SCALE * (dot_wide(gn_ref[...], value_state, 1, 1) + grad_den * ks.whole[...]) * sq_ref[...]
    qs.src[pl.ds(0, 128)] = dot_exact_left(feat_ref[...], sk_ref[...], 0, 0)
    qs.src[pl.ds(128, 128)] = dot_exact_left(feat_ref[...], grad_q, 0, 0)
    in_ref[...] = dot_exact_right(grad_q, wq_ref[...], 1, 1)
    scatter(plane, qs.src, qs.got, QS1)

    gs.last[...] = take(gs.got2, GS2)
    gather(column, gs.last, gs.whole, GS3)

    wait(others_of(r_near), recv_sem.at[RA])

    def order_terms(g, carry):
        block = r_near[:, g].reshape(256, 256)
        r_far[pl.ds(g * 8, 8)] = dot(to_natural, block).astype(BF16).reshape(8, 32, 256)
        return carry

    lax.fori_loop(0, 8, order_terms, 0)
    give(far, lambda i: r_far.at[i], r_got, RB)
    r_got[far.me] = r_far[far.me]
    gk.mid[...] = take(gk.got, GK1)
    share(plane, gk.mid, gk.got2, GK2)

    wait(all_rows(gs.whole, column), recv_sem.at[GS3])
    grad_state = gs.whole[...]
    grad_k = dot_wide(v_ref[...], grad_state, 1, 1) * sk_ref[...]
    vg_ref[...] = grad_k
    pv.src[pl.ds(0, 128)] = dot_exact_left(feat_ref[...], grad_k, 0, 0)
    grad_v = gn_ref[...] + dot_wide(mk_ref[...], grad_state)
    pv.src[pl.ds(128, 128)] = dot_exact_left(feat_ref[...], grad_v, 0, 0)
    scatter(plane, pv.src, pv.got, PV1)
    in_ref[...] += dot_exact_right(grad_v, wv_ref[...], 1, 1)

    qs.mid[...] = take(qs.got, QS1)
    share(column, qs.mid, qs.got2, QS2)

    wait(others_of(f_far), recv_sem.at[FB])
    live = jnp.where(column_rows[...] >= 0, 1.0, 0.0)
    total = jnp.zeros((128, 128), F32)
    for r in range(4):
        rows = jnp.zeros((128, 128), F32)
        for n in range(4):
            term = dot(vals_ref[0, r, n], ext[col_ref[0, r, n]])
            rows = rows + term * live[r * 4 + n : r * 4 + n + 1]
        total = total + dot_exact_right(rows, cot_ref[pl.ds(r * 128, 128)], 0, 0)
    gg.src[...] = total
    scatter(column, gg.src, gg.got, GG1)

    pv.mid[...] = take(pv.got, PV1)
    share(column, pv.mid, pv.got2, PV2)

    grad_ksum = take(gk.got2, GK2)
    gk.whole[...] = grad_ksum
    in_ref[...] += dot_exact_right(vg_ref[...] + grad_ksum * sk_ref[...], wk_ref[...], 1, 1)
    slopes = take(qs.got2, QS2)
    qs.last[...] = slopes
    gather(plane, qs.last, qs.whole, QS3)
    gg.mid[...] = take(gg.got, GG1)
    share(plane, gg.mid, gg.got2, GG2)

    chunk = take(pv.got2, PV2)
    pv.last[...] = jnp.where(plane.me < 16, chunk + slopes * gk.whole[...], chunk)
    gather(plane, pv.last, pv.whole, PV3)

    gg.last[...] = take(gg.got2, GG2)
    gather(column, gg.last, gg.whole, GG3)

    wait(others_of(r_got), recv_sem.at[RB])

    def order_back(g, carry):
        block = r_got[pl.ds(g * 8, 8)].reshape(256, 256)
        r_rows[:, g] = dot(to_wire, block).astype(BF16).reshape(8, 32, 256)
        return carry

    lax.fori_loop(0, 8, order_back, 0)
    sums = jnp.zeros((256, 512), F32)
    for a in range(8):
        sums = sums + dot(r_rows[a].reshape(256, 256), onehot[a].reshape(256, 512), 0, 0)
    returned = (sums[:128] + sums[128:]).T
    out_ref[...] = (in_ref[...] + own[...].reshape(512, 128) + returned).astype(BF16)

    wait(all_rows(qs.whole, plane), recv_sem.at[QS3])
    sums_ref[0] = qs.whole[pl.ds(128, 128)] * (1.0 / NODES)
    wait(all_rows(pv.whole, plane), recv_sem.at[PV3])
    sums_ref[1] = pv.whole[pl.ds(0, 128)] * (1.0 / NODES)
    sums_ref[2] = pv.whole[pl.ds(128, 128)] * (1.0 / NODES)
    wait(all_rows(gg.whole, column), recv_sem.at[GG3])
    sums_ref[3] = gg.whole[...] * (1.0 / NODES)
    for span, which in pending:
        wait(span, send_sem.at[which])


def shards(
    features, cotangent, w_query, w_key, w_value, w_graph, send_rows, block_col, block_count, block_vals
):
    vmem = pl.BlockSpec(memory_space=pltpu.VMEM)
    smem = pl.BlockSpec(memory_space=pltpu.SMEM)
    wide = pltpu.VMEM((512, 128), F32)
    scratch = (
        [wide] * 9
        + row_buffers()
        + row_buffers()
        + sum_buffers(128, 16, 32)
        + sum_buffers(128, 16, 32)
        + sum_buffers(128, 16, 32)
        + sum_buffers(256, 32, 16)
        + sum_buffers(256, 32, 16)
        + [
            pltpu.VMEM((8, 8, 32, 512), BF16),
            pltpu.VMEM((8, 8, 32, 128), BF16),
            pltpu.VMEM((8, 8, 32, 128), BF16),
            pltpu.VMEM((64, 32, 128), BF16),
            pltpu.VMEM((20, 128, 128), BF16),
            pltpu.VMEM((16, 128), jnp.int32),
            pltpu.VMEM((16, 128, 128), F32),
            pltpu.VMEM((4, 128, 128), F32),
            pltpu.VMEM((16, 128, 256), BF16),
            pltpu.VMEM((8, 8, 32, 256), BF16),
            pltpu.VMEM((8, 8, 32, 256), BF16),
            pltpu.VMEM((64, 32, 256), BF16),
            pltpu.VMEM((64, 32, 256), BF16),
            pltpu.VMEM((8, 8, 32, 256), BF16),
            pltpu.SemaphoreType.DMA((EXCHANGES,)),
            pltpu.SemaphoreType.DMA((EXCHANGES,)),
        ]
    )
    grad_features, sums = pl.pallas_call(
        layer_kernel,
        out_shape=(
            jax.ShapeDtypeStruct((512, 128), BF16),
            jax.ShapeDtypeStruct((4, 128, 128), F32),
        ),
        in_specs=[vmem] * 7 + [smem] + [vmem] * 3,
        out_specs=(vmem, vmem),
        scratch_shapes=scratch,
        compiler_params=pltpu.CompilerParams(
            collective_id=0, has_side_effects=True, vmem_limit_bytes=48 << 20
        ),
        name="layer",
    )(
        features, cotangent, w_query, w_key, w_value, w_graph, send_rows, block_col, block_col,
        block_count, block_vals,
    )
    return grad_features, sums[0], sums[1], sums[2], sums[3]


def solution(mesh):
    both = ("dom", "sub")
    return jax.shard_map(
        shards,
        mesh=mesh,
        in_specs=(
            P(both, None), P(both, None), P(), P(), P(), P(),
            P(both, None, None), P(both, None, None), P(both, None), P(both, None, None, None, None),
        ),
        out_specs=(P(both, None), P(), P(), P(), P()),
        check_vma=False,
    )
```

```python
import jax
import jax.numpy as jnp
from jax import lax
from jax.experimental import pallas as pl
from jax.experimental.pallas import tpu as pltpu
from jax.sharding import PartitionSpec as P

MESH = pl.DeviceIdType.MESH
F32 = jnp.float32
BF16 = jnp.bfloat16
NODES = 262144
SCALE = 1.0 / (NODES * 128)

KS1, KS2, VS1, VS2, VS3, GS1, GS2, GS3, GK1, GK2 = range(10)
PV1, PV2, PV3, QS1, QS2, QS3, GG1, GG2, GG3 = range(10, 19)
FA, FB, RA, RB = range(19, 23)
EXCHANGES = 23


def place():
    dom = lax.axis_index("dom")
    return dom // 16, (dom // 2) % 8, dom % 2, lax.axis_index("sub")


class Group:
    def __init__(self, count, me, member):
        self.count, self.me, self.member = count, me, member

    def others(self, act, first=1, stride=1):
        def body(step, carry):
            act((self.me + first + step * stride) % self.count)
            return carry

        lax.fori_loop(0, -(-(self.count - first) // stride), body, 0)


def groups():
    y, z, core, x = place()
    plane = Group(32, z * 4 + x, lambda i: ((y * 8 + i // 4) * 2 + core, i % 4))
    column = Group(16, y * 2 + core, lambda i: (i // 2 * 16 + z * 2 + i % 2, x))
    near = Group(8, core * 4 + x, lambda i: ((y * 8 + z) * 2 + i // 4, i % 4))
    far = Group(64, y * 8 + z, lambda i: (i * 2 + core, x))
    return plane, column, near, far


def split(wide):
    high = wide.astype(BF16)
    return high, (wide - high.astype(F32)).astype(BF16)


def dot(left, right, left_dim=1, right_dim=0):
    return lax.dot_general(
        left, right, (((left_dim,), (right_dim,)), ((), ())), preferred_element_type=F32
    )


def dot_wide(left, right, left_dim=1, right_dim=0):
    left_high, left_low = split(left)
    right_high, right_low = split(right)
    return (
        dot(left_high, right_high, left_dim, right_dim)
        + dot(left_high, right_low, left_dim, right_dim)
        + dot(left_low, right_high, left_dim, right_dim)
    )


def dot_exact_left(left, right, left_dim=1, right_dim=0):
    high, low = split(right)
    return dot(left, high, left_dim, right_dim) + dot(left, low, left_dim, right_dim)


def dot_exact_right(left, right, left_dim=1, right_dim=0):
    high, low = split(left)
    return dot(high, right, left_dim, right_dim) + dot(low, right, left_dim, right_dim)


class Sum:
    def __init__(self, src, got, mid, got2, last, whole):
        self.src, self.got, self.mid, self.got2, self.last, self.whole = src, got, mid, got2, last, whole


def sum_buffers(rows, first, second):
    step = rows // first
    return [
        pltpu.VMEM((rows, 128), F32),
        pltpu.VMEM((first, step, 128), F32),
        pltpu.VMEM((step, 128), F32),
        pltpu.VMEM((second, step, 128), F32),
        pltpu.VMEM((step, 128), F32),
        pltpu.VMEM((rows, 128), F32),
    ]


def row_buffers():
    return [
        pltpu.VMEM((1, 128), F32),
        pltpu.VMEM((16, 1, 128), F32),
        pltpu.VMEM((1, 128), F32),
        pltpu.VMEM((32, 1, 128), F32),
        pltpu.VMEM((1, 128), F32),
        pltpu.VMEM((1, 128), F32),
    ]


def layer_kernel(
    feat_in, cot_in, wq_in, wk_in, wv_in, wg_in, rows_in, vals_in, col_ref, cols_ref, count_ref,
    out_ref, sums_ref, *scratch
):
    places = scratch[-9:-1]
    sources = (feat_in, wk_in, wv_in, rows_in, cot_in, wg_in, vals_in, wq_in)
    copies = [pltpu.make_async_copy(a, b, scratch[-1].at[i]) for i, (a, b) in enumerate(zip(sources, places))]
    for copy in copies:
        copy.start()
    feat_ref, wk_ref, wv_ref, rows_ref, cot_ref, wg_ref, vals_ref, wq_ref = places
    (mk_ref, sk_ref, v_ref, mq_ref, sq_ref, gn_ref, inverse_ref, vg_ref, in_ref) = scratch[:9]
    ks, gk, vs, gs, gg, pv, qs = (Sum(*scratch[9 + 6 * i : 15 + 6 * i]) for i in range(7))
    (onehot, picked, f_out, f_near, f_far, ext, column_rows, contrib, own, b_src, r_out, r_near, r_far, r_got, r_rows,
     send_sem, recv_sem, rows_by, rows_to) = scratch[51:-9]

    plane, column, near, far = groups()
    barrier = pltpu.get_barrier_semaphore()

    def greet(dom, sub):
        pl.semaphore_signal(barrier, inc=1, device_id=(dom, sub), device_id_type=MESH)

    y, z, core, x = place()
    column.others(lambda i: greet(*column.member(i)))
    plane.others(lambda i: greet(*plane.member(i)))
    Group(4, x, None).others(lambda i: greet((y * 8 + z) * 2 + 1 - core, i))
    Group(8, y, None).others(
        lambda to_y: Group(8, z, None).others(lambda to_z: greet((to_y * 8 + to_z) * 2 + core, x))
    )

    pending = []

    def push(group, source, target, which, span, first=1, stride=1):
        def act(i):
            pltpu.make_async_remote_copy(
                src_ref=source(i),
                dst_ref=target,
                send_sem=send_sem.at[which],
                recv_sem=recv_sem.at[which],
                device_id=group.member(i),
                device_id_type=MESH,
            ).start()

        group.others(act, first, stride)
        if first == 1:
            pending.append((span, which))

    def wait(span, sem):
        pltpu.make_async_copy(span, span, sem).wait()

    def others_of(ref):
        return ref.at[pl.ds(0, ref.shape[0] - 1)]

    def all_rows(ref, group):
        step = ref.shape[0] // group.count
        return ref.at[pl.ds(0, ref.shape[0] - step)]

    def give(group, source, got, which, first=1, stride=1):
        push(group, source, got.at[group.me], which, others_of(got), first, stride)

    def take(got, which):
        wait(others_of(got), recv_sem.at[which])
        return jnp.sum(got[...], axis=0)

    def block_of(ref, group, i):
        step = ref.shape[0] // group.count
        return ref.at[pl.ds(pl.multiple_of(i * step, step), step)]

    def scatter(group, src, got, which):
        give(group, lambda i: block_of(src, group, i), got, which)
        got[group.me] = block_of(src, group, group.me)[...]

    def share(group, src, got, which):
        give(group, lambda i: src, got, which)
        got[group.me] = src[...]

    def gather(group, src, whole, which):
        push(group, lambda i: src, block_of(whole, group, group.me), which, all_rows(whole, group))
        block_of(whole, group, group.me)[...] = src[...]

    def feature_map(inner):
        low = jnp.exp(jnp.minimum(inner, 0.0))
        return jnp.where(inner > 0, inner + 1.0, low), jnp.where(inner > 0, 1.0, low)

    copies[0].wait()
    copies[1].wait()
    feat = feat_ref[...]
    mapped, slope = feature_map(dot(feat, wk_ref[...]))
    mk_ref[...] = mapped
    sk_ref[...] = slope
    ks.src[...] = jnp.sum(mapped, axis=0, keepdims=True)
    copies[2].wait()
    values = dot(feat, wv_ref[...])
    v_ref[...] = values
    vs.src[...] = dot_wide(mapped, values, 0, 0)

    copies[3].wait()
    rows_by[...] = jnp.concatenate([rows_ref[0], rows_ref[0]], axis=0).T

    for g in range(8):
        for a in range(8):
            rows_to[pl.ds(g * 64 + a * 8, 8)] = rows_by[pl.ds(g * 64 + a, 8, stride=8), :]
    lanes = rows_to[...].T
    row = lax.broadcasted_iota(jnp.int32, (512, 512), 0)
    for s in range(4):
        onehot[s] = jnp.where(row == lanes[s : s + 1], 1.0, 0.0).astype(BF16)
        picked[s] = dot(feat, onehot[s], 0, 0).T.reshape(64, 8, 128)
    for g in range(8):
        for a in range(8):
            f_out[a, g] = picked[:, g * 8 + a].reshape(32, 128).astype(BF16)

    pl.semaphore_wait(barrier, 31 + 15 + 3 + 49)
    share(column, ks.src, ks.got, KS1)
    give(near, lambda i: f_out.at[i], f_near, FA)
    f_near[near.me] = f_out[near.me]
    scatter(column, vs.src, vs.got, VS1)

    first = lax.broadcasted_iota(jnp.int32, (256, 256), 0)
    second = lax.broadcasted_iota(jnp.int32, (256, 256), 1)

    def slot_row(by_slot):
        return (by_slot & 7) * 32 + ((by_slot >> 3) & 7) * 4 + (by_slot >> 6)

    def wire_row(natural):
        return ((natural >> 2) & 7) * 32 + (natural & 3) * 8 + (natural >> 5)

    to_natural = jnp.where(second == wire_row(first), 1.0, 0.0).astype(BF16)
    to_wire = jnp.where(first == wire_row(second), 1.0, 0.0).astype(BF16)

    for copy in copies[4:]:
        copy.wait()
    graph_in = dot(cot_ref[...], wg_ref[...], 1, 1)
    for r in range(4):
        right = jnp.concatenate(split(graph_in[r * 128 : (r + 1) * 128]), axis=1)
        for n in range(4):
            term = dot(vals_ref[0, r, n], right, 0, 0)
            contrib[r * 4 + n] = term[:, :128] + term[:, 128:]

    columns = []
    for r in range(4):
        for n in range(4):
            block_at = jnp.broadcast_to(cols_ref[0, r : r + 1, n : n + 1], (1, 128))
            count = jnp.broadcast_to(count_ref[0:1, r : r + 1], (1, 128))
            columns.append(jnp.where(n < count, block_at, -1))
    column_rows[...] = jnp.concatenate(columns, axis=0)

    def column_sum(e):
        chosen = jnp.where(column_rows[...] == e, 1.0, 0.0)
        total = jnp.zeros((128, 128), F32)
        for k in range(16):
            total = total + contrib[k] * chosen[k : k + 1]
        return total

    def own_sum(e, carry):
        own[e] = column_sum(e)
        return carry

    def boundary_sum(e, carry):
        b_src[e] = jnp.concatenate(split(column_sum(e + 4)), axis=1)
        return carry

    lax.fori_loop(0, 4, own_sum, 0)
    lax.fori_loop(0, 16, boundary_sum, 0)

    for g in range(8):
        block = b_src[pl.ds(g * 2, 2)].reshape(256, 256)
        r_out[:, g] = dot(to_wire, block).astype(BF16).reshape(8, 32, 256)

    ks.mid[...] = take(ks.got, KS1)
    share(plane, ks.mid, ks.got2, KS2)
    vs.mid[...] = take(vs.got, VS1)
    share(plane, vs.mid, vs.got2, VS2)
    give(near, lambda i: r_out.at[i], r_near, RA)
    r_near[near.me] = r_out[near.me]

    mapped, slope = feature_map(dot(feat_ref[...], wq_ref[...]))
    mq_ref[...] = mapped
    sq_ref[...] = slope

    key_sum = take(ks.got2, KS2)
    ks.whole[...] = key_sum
    mapped = mq_ref[...]
    inverse = 1.0 / (1.0 + SCALE * jnp.sum(mapped * key_sum, axis=1, keepdims=True))
    inverse_ref[...] = jnp.broadcast_to(inverse, (512, 128))
    grad_num = cot_ref[...].astype(F32) * inverse
    gn_ref[...] = grad_num
    gs.src[...] = SCALE * dot_wide(mapped, grad_num, 0, 0)
    scatter(column, gs.src, gs.got, GS1)

    vs.last[...] = take(vs.got2, VS2)
    gather(column, vs.last, vs.whole, VS3)

    wait(others_of(f_near), recv_sem.at[FA])

    for g in range(8):
        block = f_near[:, g].reshape(256, 128)
        f_far[pl.ds(g * 8, 8)] = dot(to_natural, block).astype(BF16).reshape(8, 32, 128)
    here = ext.at[4 + far.me // 4, pl.ds(pl.multiple_of(far.me % 4 * 32, 32), 32)]
    push(far, lambda i: f_far.at[i], here, FB, others_of(f_far), 1, 2)
    here[...] = f_far[far.me]
    ext[pl.ds(0, 4)] = feat_ref[...].reshape(4, 128, 128)

    gs.mid[...] = take(gs.got, GS1)
    share(plane, gs.mid, gs.got2, GS2)
    push(far, lambda i: f_far.at[i], here, FB, None, 2, 2)

    wait(all_rows(vs.whole, column), recv_sem.at[VS3])
    value_state = vs.whole[...]
    mapped = mq_ref[...]
    inverse = inverse_ref[...]
    attended = (SCALE * dot_wide(mapped, value_state) + v_ref[...]) * inverse
    grad_den = -jnp.sum(cot_ref[...].astype(F32) * attended, axis=1, keepdims=True) * inverse
    gk.src[...] = SCALE * jnp.sum(grad_den * mapped, axis=0, keepdims=True)
    share(column, gk.src, gk.got, GK1)
    grad_q = SCALE * (dot_wide(gn_ref[...], value_state, 1, 1) + grad_den * ks.whole[...]) * sq_ref[...]
    qs.src[pl.ds(0, 128)] = dot_exact_left(feat_ref[...], sk_ref[...], 0, 0)
    qs.src[pl.ds(128, 128)] = dot_exact_left(feat_ref[...], grad_q, 0, 0)
    in_ref[...] = dot_exact_right(grad_q, wq_ref[...], 1, 1)
    scatter(plane, qs.src, qs.got, QS1)

    gs.last[...] = take(gs.got2, GS2)
    gather(column, gs.last, gs.whole, GS3)

    wait(others_of(r_near), recv_sem.at[RA])

    for g in range(8):
        block = r_near[:, g].reshape(256, 256)
        r_far[pl.ds(g * 8, 8)] = dot(to_natural, block).astype(BF16).reshape(8, 32, 256)
    give(far, lambda i: r_far.at[i], r_got, RB, 1, 3)
    r_got[far.me] = r_far[far.me]
    gk.mid[...] = take(gk.got, GK1)
    share(plane, gk.mid, gk.got2, GK2)

    wait(all_rows(gs.whole, column), recv_sem.at[GS3])
    grad_state = gs.whole[...]
    grad_k = dot_wide(v_ref[...], grad_state, 1, 1) * sk_ref[...]
    vg_ref[...] = grad_k
    pv.src[pl.ds(0, 128)] = dot_exact_left(feat_ref[...], grad_k, 0, 0)
    grad_v = gn_ref[...] + dot_wide(mk_ref[...], grad_state)
    pv.src[pl.ds(128, 128)] = dot_exact_left(feat_ref[...], grad_v, 0, 0)
    scatter(plane, pv.src, pv.got, PV1)
    in_ref[...] += dot_exact_right(grad_v, wv_ref[...], 1, 1)

    wait(others_of(f_far), recv_sem.at[FB])
    live = jnp.where(column_rows[...] >= 0, 1.0, 0.0)
    total = jnp.zeros((128, 128), F32)
    for r in range(4):
        rows = jnp.zeros((128, 128), F32)
        for n in range(4):
            term = dot(vals_ref[0, r, n], ext[col_ref[0, r, n]])
            rows = rows + term * live[r * 4 + n : r * 4 + n + 1]
        total = total + dot_exact_right(rows, cot_ref[pl.ds(r * 128, 128)], 0, 0)
    gg.src[...] = total
    scatter(column, gg.src, gg.got, GG1)
    give(far, lambda i: r_far.at[i], r_got, RB, 2, 3)
    qs.mid[...] = take(qs.got, QS1)
    share(column, qs.mid, qs.got2, QS2)

    pv.mid[...] = take(pv.got, PV1)
    share(column, pv.mid, pv.got2, PV2)
    gg.mid[...] = take(gg.got, GG1)
    share(plane, gg.mid, gg.got2, GG2)
    give(far, lambda i: r_far.at[i], r_got, RB, 3, 3)

    grad_ksum = take(gk.got2, GK2)
    gk.whole[...] = grad_ksum
    in_ref[...] += dot_exact_right(vg_ref[...] + grad_ksum * sk_ref[...], wk_ref[...], 1, 1)
    slopes = take(qs.got2, QS2)
    qs.last[...] = slopes
    chunk = take(pv.got2, PV2)
    pv.last[...] = jnp.where(plane.me < 16, chunk + slopes * gk.whole[...], chunk)
    gather(plane, pv.last, pv.whole, PV3)
    gather(plane, qs.last, qs.whole, QS3)

    gg.last[...] = take(gg.got2, GG2)
    gather(column, gg.last, gg.whole, GG3)

    wait(others_of(r_got), recv_sem.at[RB])

    to_slots = jnp.where(second == slot_row(first), 1.0, 0.0).astype(BF16)
    for g in range(8):
        block = r_got[pl.ds(g * 8, 8)].reshape(256, 256)
        r_rows[:, g] = dot(to_slots, block).astype(BF16).reshape(4, 64, 256)
    sums = jnp.zeros((512, 256), F32)
    for s in range(4):
        sums = sums + dot(onehot[s], r_rows[s].reshape(512, 256))
    returned = sums[:, :128] + sums[:, 128:]
    out_ref[...] = (in_ref[...] + own[...].reshape(512, 128) + returned).astype(BF16)

    wait(all_rows(qs.whole, plane), recv_sem.at[QS3])
    sums_ref[0] = qs.whole[pl.ds(128, 128)] * (1.0 / NODES)
    wait(all_rows(pv.whole, plane), recv_sem.at[PV3])
    sums_ref[1] = pv.whole[pl.ds(0, 128)] * (1.0 / NODES)
    sums_ref[2] = pv.whole[pl.ds(128, 128)] * (1.0 / NODES)
    wait(all_rows(gg.whole, column), recv_sem.at[GG3])
    sums_ref[3] = gg.whole[...] * (1.0 / NODES)
    for span, which in pending:
        wait(span, send_sem.at[which])


def shards(
    features, cotangent, w_query, w_key, w_value, w_graph, send_rows, block_col, block_count, block_vals
):
    vmem = pl.BlockSpec(memory_space=pltpu.VMEM)
    smem = pl.BlockSpec(memory_space=pltpu.SMEM)
    anywhere = pl.BlockSpec(memory_space=pltpu.HBM)
    wide = pltpu.VMEM((512, 128), F32)
    scratch = (
        [wide] * 9
        + row_buffers()
        + row_buffers()
        + sum_buffers(128, 16, 32)
        + sum_buffers(128, 16, 32)
        + sum_buffers(128, 16, 32)
        + sum_buffers(256, 32, 16)
        + sum_buffers(256, 32, 16)
        + [
            pltpu.VMEM((4, 512, 512), BF16),
            pltpu.VMEM((4, 64, 8, 128), F32),
            pltpu.VMEM((8, 8, 32, 128), BF16),
            pltpu.VMEM((8, 8, 32, 128), BF16),
            pltpu.VMEM((64, 32, 128), BF16),
            pltpu.VMEM((20, 128, 128), BF16),
            pltpu.VMEM((16, 128), jnp.int32),
            pltpu.VMEM((16, 128, 128), F32),
            pltpu.VMEM((4, 128, 128), F32),
            pltpu.VMEM((16, 128, 256), BF16),
            pltpu.VMEM((8, 8, 32, 256), BF16),
            pltpu.VMEM((8, 8, 32, 256), BF16),
            pltpu.VMEM((64, 32, 256), BF16),
            pltpu.VMEM((64, 32, 256), BF16),
            pltpu.VMEM((4, 8, 64, 256), BF16),
            pltpu.SemaphoreType.DMA((EXCHANGES,)),
            pltpu.SemaphoreType.DMA((EXCHANGES,)),
            pltpu.VMEM((512, 8), jnp.int32),
            pltpu.VMEM((512, 8), jnp.int32),
            pltpu.VMEM((512, 128), BF16),
            pltpu.VMEM((128, 128), BF16),
            pltpu.VMEM((128, 128), BF16),
            pltpu.VMEM((1, 4, 512), jnp.int32),
            pltpu.VMEM((512, 128), BF16),
            pltpu.VMEM((128, 128), BF16),
            pltpu.VMEM((1, 4, 4, 128, 128), BF16),
            pltpu.VMEM((128, 128), BF16),
            pltpu.SemaphoreType.DMA((8,)),
        ]
    )
    grad_features, sums = pl.pallas_call(
        layer_kernel,
        out_shape=(
            jax.ShapeDtypeStruct((512, 128), BF16),
            jax.ShapeDtypeStruct((4, 128, 128), F32),
        ),
        in_specs=[anywhere] * 8 + [smem, vmem, vmem],
        out_specs=(vmem, vmem),
        scratch_shapes=scratch,
        compiler_params=pltpu.CompilerParams(
            collective_id=0, has_side_effects=True, vmem_limit_bytes=60 << 20
        ),
        name="layer",
    )(
        features, cotangent, w_query, w_key, w_value, w_graph, jnp.swapaxes(send_rows, 1, 2), block_vals,
        block_col, block_col, block_count,
    )
    return grad_features, sums[0], sums[1], sums[2], sums[3]


def solution(mesh):
    both = ("dom", "sub")
    return jax.shard_map(
        shards,
        mesh=mesh,
        in_specs=(
            P(both, None), P(both, None), P(), P(), P(), P(),
            P(both, None, None), P(both, None, None), P(both, None), P(both, None, None, None, None),
        ),
        out_specs=(P(both, None), P(), P(), P(), P()),
        check_vma=False,
    )
```

```python
import jax
import jax.numpy as jnp
from jax import lax
from jax.experimental import pallas as pl
from jax.experimental.pallas import tpu as pltpu
from jax.sharding import PartitionSpec as P

MESH = pl.DeviceIdType.MESH
F32 = jnp.float32
BF16 = jnp.bfloat16
NODES = 262144
SCALE = 1.0 / (NODES * 128)

KS1, KS2, VS1, VS2, VS3, GS1, GS2, GS3, GK1, GK2 = range(10)
PV1, PV2, PV3, QS1, QS2, QS3, GG1, GG2, GG3 = range(10, 19)
FA, FB, RA, RB = range(19, 23)
EXCHANGES = 23


def place():
    dom = lax.axis_index("dom")
    return dom // 16, (dom // 2) % 8, dom % 2, lax.axis_index("sub")


class Group:
    def __init__(self, count, me, member):
        self.count, self.me, self.member = count, me, member

    def others(self, act, first=1, stride=1):
        def body(step, carry):
            act((self.me + first + step * stride) % self.count)
            return carry

        lax.fori_loop(0, -(-(self.count - first) // stride), body, 0)


def groups():
    y, z, core, x = place()
    plane = Group(32, z * 4 + x, lambda i: ((y * 8 + i // 4) * 2 + core, i % 4))
    column = Group(16, y * 2 + core, lambda i: (i // 2 * 16 + z * 2 + i % 2, x))
    near = Group(8, core * 4 + x, lambda i: ((y * 8 + z) * 2 + i // 4, i % 4))
    far = Group(64, y * 8 + z, lambda i: (i * 2 + core, x))
    return plane, column, near, far


def split(wide):
    high = wide.astype(BF16)
    return high, (wide - high.astype(F32)).astype(BF16)


def dot(left, right, left_dim=1, right_dim=0):
    return lax.dot_general(
        left, right, (((left_dim,), (right_dim,)), ((), ())), preferred_element_type=F32
    )


def dot_wide(left, right, left_dim=1, right_dim=0):
    left_high, left_low = split(left)
    right_high, right_low = split(right)
    return (
        dot(left_high, right_high, left_dim, right_dim)
        + dot(left_high, right_low, left_dim, right_dim)
        + dot(left_low, right_high, left_dim, right_dim)
    )


def dot_exact_left(left, right, left_dim=1, right_dim=0):
    high, low = split(right)
    return dot(left, high, left_dim, right_dim) + dot(left, low, left_dim, right_dim)


def dot_exact_right(left, right, left_dim=1, right_dim=0):
    high, low = split(left)
    return dot(high, right, left_dim, right_dim) + dot(low, right, left_dim, right_dim)


class Sum:
    def __init__(self, src, got, mid, got2, last, whole):
        self.src, self.got, self.mid, self.got2, self.last, self.whole = src, got, mid, got2, last, whole


def sum_buffers(rows, first, second):
    step = rows // first
    return [
        pltpu.VMEM((rows, 128), F32),
        pltpu.VMEM((first, step, 128), F32),
        pltpu.VMEM((step, 128), F32),
        pltpu.VMEM((second, step, 128), F32),
        pltpu.VMEM((step, 128), F32),
        pltpu.VMEM((rows, 128), F32),
    ]


def row_buffers(first, second):
    return [
        pltpu.VMEM((first, 128), F32),
        pltpu.VMEM((16, first, 128), F32),
        pltpu.VMEM((second, 128), F32),
        pltpu.VMEM((32, second, 128), F32),
        pltpu.VMEM((1, 128), F32),
        pltpu.VMEM((1, 128), F32),
    ]


def layer_kernel(
    feat_in, cot_in, wq_in, wk_in, wv_in, wg_in, rows_in, vals_in, col_ref, cols_ref, count_ref,
    out_ref, sums_ref, *scratch
):
    places = scratch[-9:-1]
    sources = (feat_in, wk_in, wv_in, rows_in, cot_in, wg_in, vals_in, wq_in)
    copies = [pltpu.make_async_copy(a, b, scratch[-1].at[i]) for i, (a, b) in enumerate(zip(sources, places))]
    for copy in copies:
        copy.start()
    feat_ref, wk_ref, wv_ref, rows_ref, cot_ref, wg_ref, vals_ref, wq_ref = places
    (mk_ref, sk_ref, v_ref, mq_ref, sq_ref, gn_ref, inverse_ref, vg_ref, in_ref) = scratch[:9]
    ks, gk, vs, gs, gg, pv, qs = (Sum(*scratch[9 + 6 * i : 15 + 6 * i]) for i in range(7))
    (onehot, picked, f_out, f_near, f_far, ext, column_rows, contrib, own, b_src, r_out, r_near, r_far, r_got, r_rows,
     send_sem, recv_sem, rows_by, rows_to) = scratch[51:-9]

    plane, column, near, far = groups()
    barrier = pltpu.get_barrier_semaphore()

    def greet(dom, sub):
        pl.semaphore_signal(barrier, inc=1, device_id=(dom, sub), device_id_type=MESH)

    y, z, core, x = place()
    column.others(lambda i: greet(*column.member(i)))
    plane.others(lambda i: greet(*plane.member(i)))
    Group(4, x, None).others(lambda i: greet((y * 8 + z) * 2 + 1 - core, i))
    Group(8, y, None).others(
        lambda to_y: Group(8, z, None).others(lambda to_z: greet((to_y * 8 + to_z) * 2 + core, x))
    )

    pending = []

    def push(group, source, target, which, span, first=1, stride=1):
        def act(i):
            pltpu.make_async_remote_copy(
                src_ref=source(i),
                dst_ref=target,
                send_sem=send_sem.at[which],
                recv_sem=recv_sem.at[which],
                device_id=group.member(i),
                device_id_type=MESH,
            ).start()

        group.others(act, first, stride)
        if first == 1:
            pending.append((span, which))

    def wait(span, sem):
        pltpu.make_async_copy(span, span, sem).wait()

    def others_of(ref):
        return ref.at[pl.ds(0, ref.shape[0] - 1)]

    def all_rows(ref, group):
        step = ref.shape[0] // group.count
        return ref.at[pl.ds(0, ref.shape[0] - step)]

    def give(group, source, got, which, first=1, stride=1):
        push(group, source, got.at[group.me], which, others_of(got), first, stride)

    def take(got, which):
        wait(others_of(got), recv_sem.at[which])
        return jnp.sum(got[...], axis=0)

    def block_of(ref, group, i):
        step = ref.shape[0] // group.count
        return ref.at[pl.ds(pl.multiple_of(i * step, step), step)]

    def scatter(group, src, got, which):
        give(group, lambda i: block_of(src, group, i), got, which)
        got[group.me] = block_of(src, group, group.me)[...]

    def share(group, src, got, which):
        give(group, lambda i: src, got, which)
        got[group.me] = src[...]

    def gather(group, src, whole, which):
        push(group, lambda i: src, block_of(whole, group, group.me), which, all_rows(whole, group))
        block_of(whole, group, group.me)[...] = src[...]

    def feature_map(inner):
        low = jnp.exp(jnp.minimum(inner, 0.0))
        return jnp.where(inner > 0, inner + 1.0, low), jnp.where(inner > 0, 1.0, low)

    copies[0].wait()
    copies[1].wait()
    feat = feat_ref[...]
    mapped, slope = feature_map(dot(feat, wk_ref[...]))
    mk_ref[...] = mapped
    sk_ref[...] = slope
    ks.src[...] = jnp.sum(mapped, axis=0, keepdims=True)
    copies[2].wait()
    values = dot(feat, wv_ref[...])
    v_ref[...] = values
    vs.src[...] = dot_wide(mapped, values, 0, 0)

    copies[3].wait()
    rows_by[...] = jnp.concatenate([rows_ref[0], rows_ref[0]], axis=0).T

    for g in range(8):
        for a in range(8):
            rows_to[pl.ds(g * 64 + a * 8, 8)] = rows_by[pl.ds(g * 64 + a, 8, stride=8), :]
    lanes = rows_to[...].T
    row = lax.broadcasted_iota(jnp.int32, (512, 512), 0)
    for s in range(4):
        onehot[s] = jnp.where(row == lanes[s : s + 1], 1.0, 0.0).astype(BF16)
        picked[s] = dot(feat, onehot[s], 0, 0).T.reshape(64, 8, 128)
    for g in range(8):
        for a in range(8):
            f_out[a, g] = picked[:, g * 8 + a].reshape(32, 128).astype(BF16)

    pl.semaphore_wait(barrier, 31 + 15 + 3 + 49)
    share(column, ks.src, ks.got, KS1)
    give(near, lambda i: f_out.at[i], f_near, FA)
    f_near[near.me] = f_out[near.me]
    scatter(column, vs.src, vs.got, VS1)

    first = lax.broadcasted_iota(jnp.int32, (256, 256), 0)
    second = lax.broadcasted_iota(jnp.int32, (256, 256), 1)

    def slot_row(by_slot):
        return (by_slot & 7) * 32 + ((by_slot >> 3) & 7) * 4 + (by_slot >> 6)

    def wire_row(natural):
        return ((natural >> 2) & 7) * 32 + (natural & 3) * 8 + (natural >> 5)

    to_natural = jnp.where(second == wire_row(first), 1.0, 0.0).astype(BF16)
    to_wire = jnp.where(first == wire_row(second), 1.0, 0.0).astype(BF16)

    for copy in copies[4:]:
        copy.wait()
    graph_in = dot(cot_ref[...], wg_ref[...], 1, 1)
    for r in range(4):
        right = jnp.concatenate(split(graph_in[r * 128 : (r + 1) * 128]), axis=1)
        for n in range(4):
            term = dot(vals_ref[0, r, n], right, 0, 0)
            contrib[r * 4 + n] = term[:, :128] + term[:, 128:]

    columns = []
    for r in range(4):
        for n in range(4):
            block_at = jnp.broadcast_to(cols_ref[0, r : r + 1, n : n + 1], (1, 128))
            count = jnp.broadcast_to(count_ref[0:1, r : r + 1], (1, 128))
            columns.append(jnp.where(n < count, block_at, -1))
    column_rows[...] = jnp.concatenate(columns, axis=0)

    def column_sum(e):
        chosen = jnp.where(column_rows[...] == e, 1.0, 0.0)
        total = jnp.zeros((128, 128), F32)
        for k in range(16):
            total = total + contrib[k] * chosen[k : k + 1]
        return total

    def own_sum(e, carry):
        own[e] = column_sum(e)
        return carry

    def boundary_sum(e, largest):
        terms = column_sum(e + 4)
        b_src[e] = jnp.concatenate(split(terms), axis=1)
        return jnp.maximum(largest, jnp.max(jnp.abs(terms), axis=0, keepdims=True))

    lax.fori_loop(0, 4, own_sum, 0)
    largest = lax.fori_loop(0, 16, boundary_sum, jnp.zeros((1, 128), F32))

    for g in range(8):
        block = b_src[pl.ds(g * 2, 2)].reshape(256, 256)
        r_out[:, g] = dot(to_wire, block).astype(BF16).reshape(8, 32, 256)

    ks.mid[pl.ds(0, 1)] = take(ks.got, KS1)
    ks.mid[pl.ds(1, 1)] = jnp.broadcast_to(jnp.max(largest, axis=1, keepdims=True), (1, 128))
    share(plane, ks.mid, ks.got2, KS2)
    vs.mid[...] = take(vs.got, VS1)
    share(plane, vs.mid, vs.got2, VS2)
    give(near, lambda i: r_out.at[i], r_near, RA)
    r_near[near.me] = r_out[near.me]

    mapped, slope = feature_map(dot(feat_ref[...], wq_ref[...]))
    mq_ref[...] = mapped
    sq_ref[...] = slope

    key_sum = take(ks.got2, KS2)[0:1]
    ks.whole[...] = key_sum
    mapped = mq_ref[...]
    inverse = 1.0 / (1.0 + SCALE * jnp.sum(mapped * key_sum, axis=1, keepdims=True))
    inverse_ref[...] = jnp.broadcast_to(inverse, (512, 128))
    grad_num = cot_ref[...].astype(F32) * inverse
    gn_ref[...] = grad_num
    gs.src[...] = SCALE * dot_wide(mapped, grad_num, 0, 0)
    scatter(column, gs.src, gs.got, GS1)

    vs.last[...] = take(vs.got2, VS2)
    gather(column, vs.last, vs.whole, VS3)

    wait(others_of(f_near), recv_sem.at[FA])

    for g in range(8):
        block = f_near[:, g].reshape(256, 128)
        f_far[pl.ds(g * 8, 8)] = dot(to_natural, block).astype(BF16).reshape(8, 32, 128)
    here = ext.at[4 + far.me // 4, pl.ds(pl.multiple_of(far.me % 4 * 32, 32), 32)]
    push(far, lambda i: f_far.at[i], here, FB, others_of(f_far), 1, 2)
    here[...] = f_far[far.me]
    ext[pl.ds(0, 4)] = feat_ref[...].reshape(4, 128, 128)

    gs.mid[...] = take(gs.got, GS1)
    share(plane, gs.mid, gs.got2, GS2)
    push(far, lambda i: f_far.at[i], here, FB, None, 2, 2)

    wait(all_rows(vs.whole, column), recv_sem.at[VS3])
    value_state = vs.whole[...]
    mapped = mq_ref[...]
    inverse = inverse_ref[...]
    attended = (SCALE * dot_wide(mapped, value_state) + v_ref[...]) * inverse
    grad_den = -jnp.sum(cot_ref[...].astype(F32) * attended, axis=1, keepdims=True) * inverse
    gk.src[pl.ds(0, 1)] = SCALE * jnp.sum(grad_den * mapped, axis=0, keepdims=True)
    gk.src[pl.ds(1, 1)] = jnp.max(ks.got2[...], axis=0)[1:2]
    share(column, gk.src, gk.got, GK1)
    grad_q = SCALE * (dot_wide(gn_ref[...], value_state, 1, 1) + grad_den * ks.whole[...]) * sq_ref[...]
    qs.src[pl.ds(0, 128)] = dot_exact_left(feat_ref[...], sk_ref[...], 0, 0)
    qs.src[pl.ds(128, 128)] = dot_exact_left(feat_ref[...], grad_q, 0, 0)
    in_ref[...] = dot_exact_right(grad_q, wq_ref[...], 1, 1)
    scatter(plane, qs.src, qs.got, QS1)

    gs.last[...] = take(gs.got2, GS2)
    gather(column, gs.last, gs.whole, GS3)

    gk.mid[...] = take(gk.got, GK1)[0:1]
    top = jnp.maximum(jnp.max(gk.got[...], axis=0)[1:2], 1e-30)
    to_code = 1.0 / top
    from_code = top * (1.0 / (32767.0 * 32767.0))
    wait(others_of(r_near), recv_sem.at[RA])

    for g in range(8):
        block = r_near[:, g].reshape(256, 256)
        terms = dot(to_natural, block)
        terms = terms[:, :128] + terms[:, 128:]
        code = jnp.minimum(jnp.sqrt(jnp.abs(terms) * to_code) * 32767.0 + 0.5, 32767.0)
        code = jnp.where(terms < 0, -code, code).astype(jnp.int32).astype(jnp.int16)
        r_far[pl.ds(g * 8, 8)] = code.reshape(8, 32, 128)
    give(far, lambda i: r_far.at[i], r_got, RB, 1, 2)
    r_got[far.me] = r_far[far.me]
    share(plane, gk.mid, gk.got2, GK2)

    wait(all_rows(gs.whole, column), recv_sem.at[GS3])
    grad_state = gs.whole[...]
    grad_k = dot_wide(v_ref[...], grad_state, 1, 1) * sk_ref[...]
    vg_ref[...] = grad_k
    pv.src[pl.ds(0, 128)] = dot_exact_left(feat_ref[...], grad_k, 0, 0)
    grad_v = gn_ref[...] + dot_wide(mk_ref[...], grad_state)
    pv.src[pl.ds(128, 128)] = dot_exact_left(feat_ref[...], grad_v, 0, 0)
    scatter(plane, pv.src, pv.got, PV1)
    in_ref[...] += dot_exact_right(grad_v, wv_ref[...], 1, 1)

    wait(others_of(f_far), recv_sem.at[FB])
    live = jnp.where(column_rows[...] >= 0, 1.0, 0.0)
    total = jnp.zeros((128, 128), F32)
    for r in range(4):
        rows = jnp.zeros((128, 128), F32)
        for n in range(4):
            term = dot(vals_ref[0, r, n], ext[col_ref[0, r, n]])
            rows = rows + term * live[r * 4 + n : r * 4 + n + 1]
        total = total + dot_exact_right(rows, cot_ref[pl.ds(r * 128, 128)], 0, 0)
    gg.src[...] = total
    scatter(column, gg.src, gg.got, GG1)
    give(far, lambda i: r_far.at[i], r_got, RB, 2, 2)
    qs.mid[...] = take(qs.got, QS1)
    share(column, qs.mid, qs.got2, QS2)

    pv.mid[...] = take(pv.got, PV1)
    share(column, pv.mid, pv.got2, PV2)
    gg.mid[...] = take(gg.got, GG1)
    share(plane, gg.mid, gg.got2, GG2)

    grad_ksum = take(gk.got2, GK2)
    gk.whole[...] = grad_ksum
    in_ref[...] += dot_exact_right(vg_ref[...] + grad_ksum * sk_ref[...], wk_ref[...], 1, 1)
    slopes = take(qs.got2, QS2)
    qs.last[...] = slopes
    chunk = take(pv.got2, PV2)
    pv.last[...] = jnp.where(plane.me < 16, chunk + slopes * gk.whole[...], chunk)
    gather(plane, pv.last, pv.whole, PV3)
    gather(plane, qs.last, qs.whole, QS3)

    gg.last[...] = take(gg.got2, GG2)
    gather(column, gg.last, gg.whole, GG3)

    wait(others_of(r_got), recv_sem.at[RB])

    to_slots = jnp.where(second == slot_row(first), 1.0, 0.0).astype(BF16)
    for g in range(8):
        code = r_got[pl.ds(g * 8, 8)].reshape(256, 128).astype(jnp.int32).astype(F32)
        block = jnp.concatenate(split(code * jnp.abs(code) * from_code), axis=1)
        r_rows[:, g] = dot(to_slots, block).astype(BF16).reshape(4, 64, 256)
    sums = jnp.zeros((512, 256), F32)
    for s in range(4):
        sums = sums + dot(onehot[s], r_rows[s].reshape(512, 256))
    returned = sums[:, :128] + sums[:, 128:]
    out_ref[...] = (in_ref[...] + own[...].reshape(512, 128) + returned).astype(BF16)

    wait(all_rows(qs.whole, plane), recv_sem.at[QS3])
    sums_ref[0] = qs.whole[pl.ds(128, 128)] * (1.0 / NODES)
    wait(all_rows(pv.whole, plane), recv_sem.at[PV3])
    sums_ref[1] = pv.whole[pl.ds(0, 128)] * (1.0 / NODES)
    sums_ref[2] = pv.whole[pl.ds(128, 128)] * (1.0 / NODES)
    wait(all_rows(gg.whole, column), recv_sem.at[GG3])
    sums_ref[3] = gg.whole[...] * (1.0 / NODES)
    for span, which in pending:
        wait(span, send_sem.at[which])


def shards(
    features, cotangent, w_query, w_key, w_value, w_graph, send_rows, block_col, block_count, block_vals
):
    vmem = pl.BlockSpec(memory_space=pltpu.VMEM)
    smem = pl.BlockSpec(memory_space=pltpu.SMEM)
    anywhere = pl.BlockSpec(memory_space=pltpu.HBM)
    wide = pltpu.VMEM((512, 128), F32)
    scratch = (
        [wide] * 9
        + row_buffers(1, 2)
        + row_buffers(2, 1)
        + sum_buffers(128, 16, 32)
        + sum_buffers(128, 16, 32)
        + sum_buffers(128, 16, 32)
        + sum_buffers(256, 32, 16)
        + sum_buffers(256, 32, 16)
        + [
            pltpu.VMEM((4, 512, 512), BF16),
            pltpu.VMEM((4, 64, 8, 128), F32),
            pltpu.VMEM((8, 8, 32, 128), BF16),
            pltpu.VMEM((8, 8, 32, 128), BF16),
            pltpu.VMEM((64, 32, 128), BF16),
            pltpu.VMEM((20, 128, 128), BF16),
            pltpu.VMEM((16, 128), jnp.int32),
            pltpu.VMEM((16, 128, 128), F32),
            pltpu.VMEM((4, 128, 128), F32),
            pltpu.VMEM((16, 128, 256), BF16),
            pltpu.VMEM((8, 8, 32, 256), BF16),
            pltpu.VMEM((8, 8, 32, 256), BF16),
            pltpu.VMEM((64, 32, 128), jnp.int16),
            pltpu.VMEM((64, 32, 128), jnp.int16),
            pltpu.VMEM((4, 8, 64, 256), BF16),
            pltpu.SemaphoreType.DMA((EXCHANGES,)),
            pltpu.SemaphoreType.DMA((EXCHANGES,)),
            pltpu.VMEM((512, 8), jnp.int32),
            pltpu.VMEM((512, 8), jnp.int32),
            pltpu.VMEM((512, 128), BF16),
            pltpu.VMEM((128, 128), BF16),
            pltpu.VMEM((128, 128), BF16),
            pltpu.VMEM((1, 4, 512), jnp.int32),
            pltpu.VMEM((512, 128), BF16),
            pltpu.VMEM((128, 128), BF16),
            pltpu.VMEM((1, 4, 4, 128, 128), BF16),
            pltpu.VMEM((128, 128), BF16),
            pltpu.SemaphoreType.DMA((8,)),
        ]
    )
    grad_features, sums = pl.pallas_call(
        layer_kernel,
        out_shape=(
            jax.ShapeDtypeStruct((512, 128), BF16),
            jax.ShapeDtypeStruct((4, 128, 128), F32),
        ),
        in_specs=[anywhere] * 8 + [smem, vmem, vmem],
        out_specs=(vmem, vmem),
        scratch_shapes=scratch,
        compiler_params=pltpu.CompilerParams(
            collective_id=0, has_side_effects=True, vmem_limit_bytes=60 << 20
        ),
        name="layer",
    )(
        features, cotangent, w_query, w_key, w_value, w_graph, jnp.swapaxes(send_rows, 1, 2), block_vals,
        block_col, block_col, block_count,
    )
    return grad_features, sums[0], sums[1], sums[2], sums[3]


def solution(mesh):
    both = ("dom", "sub")
    return jax.shard_map(
        shards,
        mesh=mesh,
        in_specs=(
            P(both, None), P(both, None), P(), P(), P(), P(),
            P(both, None, None), P(both, None, None), P(both, None), P(both, None, None, None, None),
        ),
        out_specs=(P(both, None), P(), P(), P(), P()),
        check_vma=False,
    )
```

```python
import jax
import jax.numpy as jnp
from jax import lax
from jax.experimental import pallas as pl
from jax.experimental.pallas import tpu as pltpu
from jax.sharding import PartitionSpec as P

MESH = pl.DeviceIdType.MESH
F32 = jnp.float32
BF16 = jnp.bfloat16
NODES = 262144
SCALE = 1.0 / (NODES * 128)

KS1, KS2, VS1, VS2, VS3, GS1, GS2, GS3, GK1, GK2 = range(10)
PV1, PV2, PV3, QS1, QS2, QS3, GG1, GG2, GG3 = range(10, 19)
FA, FB, RA, RB = range(19, 23)
EXCHANGES = 23


def place():
    dom = lax.axis_index("dom")
    return dom // 16, (dom // 2) % 8, dom % 2, lax.axis_index("sub")


class Group:
    def __init__(self, count, me, member):
        self.count, self.me, self.member = count, me, member

    def others(self, act, first=1, stride=1):
        def body(step, carry):
            act((self.me + first + step * stride) % self.count)
            return carry

        count = -(-(self.count - first) // stride)
        near_ones = self.count // 4 - 1 if stride == 1 else 0
        lax.fori_loop(near_ones, count, body, 0)
        if near_ones > 0:
            lax.fori_loop(0, near_ones, body, 0)


def groups():
    y, z, core, x = place()
    plane = Group(32, z * 4 + x, lambda i: ((y * 8 + i // 4) * 2 + core, i % 4))
    column = Group(16, y * 2 + core, lambda i: (i // 2 * 16 + z * 2 + i % 2, x))
    near = Group(8, core * 4 + x, lambda i: ((y * 8 + z) * 2 + i // 4, i % 4))
    far = Group(64, y * 8 + z, lambda i: (i * 2 + core, x))
    return plane, column, near, far


def split(wide):
    high = wide.astype(BF16)
    return high, (wide - high.astype(F32)).astype(BF16)


def dot(left, right, left_dim=1, right_dim=0):
    return lax.dot_general(
        left, right, (((left_dim,), (right_dim,)), ((), ())), preferred_element_type=F32
    )


def dot_wide(left, right, left_dim=1, right_dim=0):
    left_high, left_low = split(left)
    right_high, right_low = split(right)
    return (
        dot(left_high, right_high, left_dim, right_dim)
        + dot(left_high, right_low, left_dim, right_dim)
        + dot(left_low, right_high, left_dim, right_dim)
    )


def dot_exact_left(left, right, left_dim=1, right_dim=0):
    high, low = split(right)
    return dot(left, high, left_dim, right_dim) + dot(left, low, left_dim, right_dim)


def dot_exact_right(left, right, left_dim=1, right_dim=0):
    high, low = split(left)
    return dot(high, right, left_dim, right_dim) + dot(low, right, left_dim, right_dim)


class Sum:
    def __init__(self, src, got, mid, got2, last, whole):
        self.src, self.got, self.mid, self.got2, self.last, self.whole = src, got, mid, got2, last, whole


def sum_buffers(rows, first, second):
    step = rows // first
    return [
        pltpu.VMEM((rows, 128), F32),
        pltpu.VMEM((first, step, 128), F32),
        pltpu.VMEM((step, 128), F32),
        pltpu.VMEM((second, step, 128), F32),
        pltpu.VMEM((step, 128), F32),
        pltpu.VMEM((rows, 128), F32),
    ]


def row_buffers(first, second):
    return [
        pltpu.VMEM((first, 128), F32),
        pltpu.VMEM((16, first, 128), F32),
        pltpu.VMEM((second, 128), F32),
        pltpu.VMEM((32, second, 128), F32),
        pltpu.VMEM((1, 128), F32),
        pltpu.VMEM((1, 128), F32),
    ]


def layer_kernel(
    feat_in, cot_in, wq_in, wk_in, wv_in, wg_in, rows_in, vals_in, col_ref, cols_ref, count_ref,
    out_ref, sums_ref, *scratch
):
    places = scratch[-9:-1]
    sources = (feat_in, wk_in, wv_in, rows_in, cot_in, wg_in, vals_in, wq_in)
    copies = [pltpu.make_async_copy(a, b, scratch[-1].at[i]) for i, (a, b) in enumerate(zip(sources, places))]
    for copy in copies:
        copy.start()
    feat_ref, wk_ref, wv_ref, rows_ref, cot_ref, wg_ref, vals_ref, wq_ref = places
    (mk_ref, sk_ref, v_ref, mq_ref, sq_ref, gn_ref, inverse_ref, vg_ref, in_ref) = scratch[:9]
    ks, gk, vs, gs, gg, pv, qs = (Sum(*scratch[9 + 6 * i : 15 + 6 * i]) for i in range(7))
    (onehot, picked, f_out, f_near, f_far, ext, column_rows, contrib, own, b_src, r_out, r_near, r_far, r_got, r_rows,
     send_sem, recv_sem, rows_by, rows_to) = scratch[51:-9]

    plane, column, near, far = groups()
    barrier = pltpu.get_barrier_semaphore()

    def greet(dom, sub):
        pl.semaphore_signal(barrier, inc=1, device_id=(dom, sub), device_id_type=MESH)

    y, z, core, x = place()
    column.others(lambda i: greet(*column.member(i)))
    plane.others(lambda i: greet(*plane.member(i)))
    Group(4, x, None).others(lambda i: greet((y * 8 + z) * 2 + 1 - core, i))
    Group(8, y, None).others(
        lambda to_y: Group(8, z, None).others(lambda to_z: greet((to_y * 8 + to_z) * 2 + core, x))
    )

    pending = []

    def push(group, source, target, which, span, first=1, stride=1):
        def act(i):
            pltpu.make_async_remote_copy(
                src_ref=source(i),
                dst_ref=target,
                send_sem=send_sem.at[which],
                recv_sem=recv_sem.at[which],
                device_id=group.member(i),
                device_id_type=MESH,
            ).start()

        group.others(act, first, stride)
        if first == 1:
            pending.append((span, which))

    def wait(span, sem):
        pltpu.make_async_copy(span, span, sem).wait()

    def others_of(ref):
        return ref.at[pl.ds(0, ref.shape[0] - 1)]

    def all_rows(ref, group):
        step = ref.shape[0] // group.count
        return ref.at[pl.ds(0, ref.shape[0] - step)]

    def give(group, source, got, which, first=1, stride=1):
        push(group, source, got.at[group.me], which, others_of(got), first, stride)

    def take(got, which):
        wait(others_of(got), recv_sem.at[which])
        return jnp.sum(got[...], axis=0)

    def block_of(ref, group, i):
        step = ref.shape[0] // group.count
        return ref.at[pl.ds(pl.multiple_of(i * step, step), step)]

    def scatter(group, src, got, which):
        give(group, lambda i: block_of(src, group, i), got, which)
        got[group.me] = block_of(src, group, group.me)[...]

    def share(group, src, got, which):
        give(group, lambda i: src, got, which)
        got[group.me] = src[...]

    def gather(group, src, whole, which):
        push(group, lambda i: src, block_of(whole, group, group.me), which, all_rows(whole, group))
        block_of(whole, group, group.me)[...] = src[...]

    def feature_map(inner):
        low = jnp.exp(jnp.minimum(inner, 0.0))
        return jnp.where(inner > 0, inner + 1.0, low), jnp.where(inner > 0, 1.0, low)

    copies[0].wait()
    copies[1].wait()
    feat = feat_ref[...]
    mapped, slope = feature_map(dot(feat, wk_ref[...]))
    mk_ref[...] = mapped
    sk_ref[...] = slope
    ks.src[...] = jnp.sum(mapped, axis=0, keepdims=True)
    copies[2].wait()
    values = dot(feat, wv_ref[...])
    v_ref[...] = values
    vs.src[...] = dot_wide(mapped, values, 0, 0)

    copies[3].wait()
    rows_by[...] = jnp.concatenate([rows_ref[0], rows_ref[0]], axis=0).T

    for g in range(8):
        for a in range(8):
            rows_to[pl.ds(g * 64 + a * 8, 8)] = rows_by[pl.ds(g * 64 + a, 8, stride=8), :]
    lanes = rows_to[...].T
    row = lax.broadcasted_iota(jnp.int32, (512, 512), 0)
    for s in range(4):
        onehot[s] = jnp.where(row == lanes[s : s + 1], 1.0, 0.0).astype(BF16)
        picked[s] = dot(feat, onehot[s], 0, 0).T.reshape(64, 8, 128)
    for g in range(8):
        for a in range(8):
            f_out[a, g] = picked[:, g * 8 + a].reshape(32, 128).astype(BF16)

    pl.semaphore_wait(barrier, 31 + 15 + 3 + 49)
    share(column, ks.src, ks.got, KS1)
    give(near, lambda i: f_out.at[i], f_near, FA)
    f_near[near.me] = f_out[near.me]
    scatter(column, vs.src, vs.got, VS1)

    first = lax.broadcasted_iota(jnp.int32, (256, 256), 0)
    second = lax.broadcasted_iota(jnp.int32, (256, 256), 1)

    def slot_row(by_slot):
        return (by_slot & 7) * 32 + ((by_slot >> 3) & 7) * 4 + (by_slot >> 6)

    def wire_row(natural):
        return ((natural >> 2) & 7) * 32 + (natural & 3) * 8 + (natural >> 5)

    to_natural = jnp.where(second == wire_row(first), 1.0, 0.0).astype(BF16)
    to_wire = jnp.where(first == wire_row(second), 1.0, 0.0).astype(BF16)

    for copy in copies[4:]:
        copy.wait()
    graph_in = dot(cot_ref[...], wg_ref[...], 1, 1)
    for r in range(4):
        right = jnp.concatenate(split(graph_in[r * 128 : (r + 1) * 128]), axis=1)
        for n in range(4):
            term = dot(vals_ref[0, r, n], right, 0, 0)
            contrib[r * 4 + n] = term[:, :128] + term[:, 128:]

    columns = []
    for r in range(4):
        for n in range(4):
            block_at = jnp.broadcast_to(cols_ref[0, r : r + 1, n : n + 1], (1, 128))
            count = jnp.broadcast_to(count_ref[0:1, r : r + 1], (1, 128))
            columns.append(jnp.where(n < count, block_at, -1))
    column_rows[...] = jnp.concatenate(columns, axis=0)

    def column_sum(e):
        chosen = jnp.where(column_rows[...] == e, 1.0, 0.0)
        total = jnp.zeros((128, 128), F32)
        for k in range(16):
            total = total + contrib[k] * chosen[k : k + 1]
        return total

    def own_sum(e, carry):
        own[e] = column_sum(e)
        return carry

    def boundary_sum(e, largest):
        terms = column_sum(e + 4)
        b_src[e] = jnp.concatenate(split(terms), axis=1)
        return jnp.maximum(largest, jnp.max(jnp.abs(terms), axis=0, keepdims=True))

    lax.fori_loop(0, 4, own_sum, 0)
    largest = lax.fori_loop(0, 16, boundary_sum, jnp.zeros((1, 128), F32))

    for g in range(8):
        block = b_src[pl.ds(g * 2, 2)].reshape(256, 256)
        r_out[:, g] = dot(to_wire, block).astype(BF16).reshape(8, 32, 256)

    ks.mid[pl.ds(0, 1)] = take(ks.got, KS1)
    ks.mid[pl.ds(1, 1)] = jnp.broadcast_to(jnp.max(largest, axis=1, keepdims=True), (1, 128))
    share(plane, ks.mid, ks.got2, KS2)
    vs.mid[...] = take(vs.got, VS1)
    share(plane, vs.mid, vs.got2, VS2)
    give(near, lambda i: r_out.at[i], r_near, RA)
    r_near[near.me] = r_out[near.me]

    mapped, slope = feature_map(dot(feat_ref[...], wq_ref[...]))
    mq_ref[...] = mapped
    sq_ref[...] = slope

    key_sum = take(ks.got2, KS2)[0:1]
    ks.whole[...] = key_sum
    mapped = mq_ref[...]
    inverse = 1.0 / (1.0 + SCALE * jnp.sum(mapped * key_sum, axis=1, keepdims=True))
    inverse_ref[...] = jnp.broadcast_to(inverse, (512, 128))
    grad_num = cot_ref[...].astype(F32) * inverse
    gn_ref[...] = grad_num
    gs.src[...] = SCALE * dot_wide(mapped, grad_num, 0, 0)
    scatter(column, gs.src, gs.got, GS1)

    vs.last[...] = take(vs.got2, VS2)
    gather(column, vs.last, vs.whole, VS3)

    wait(others_of(f_near), recv_sem.at[FA])

    for g in range(8):
        block = f_near[:, g].reshape(256, 128)
        f_far[pl.ds(g * 8, 8)] = dot(to_natural, block).astype(BF16).reshape(8, 32, 128)
    here = ext.at[4 + far.me // 4, pl.ds(pl.multiple_of(far.me % 4 * 32, 32), 32)]
    push(far, lambda i: f_far.at[i], here, FB, others_of(f_far), 1, 2)
    here[...] = f_far[far.me]
    ext[pl.ds(0, 4)] = feat_ref[...].reshape(4, 128, 128)

    gs.mid[...] = take(gs.got, GS1)
    share(plane, gs.mid, gs.got2, GS2)
    push(far, lambda i: f_far.at[i], here, FB, None, 2, 2)

    wait(all_rows(vs.whole, column), recv_sem.at[VS3])
    value_state = vs.whole[...]
    mapped = mq_ref[...]
    inverse = inverse_ref[...]
    attended = (SCALE * dot_wide(mapped, value_state) + v_ref[...]) * inverse
    grad_den = -jnp.sum(cot_ref[...].astype(F32) * attended, axis=1, keepdims=True) * inverse
    gk.src[pl.ds(0, 1)] = SCALE * jnp.sum(grad_den * mapped, axis=0, keepdims=True)
    gk.src[pl.ds(1, 1)] = jnp.max(ks.got2[...], axis=0)[1:2]
    share(column, gk.src, gk.got, GK1)
    grad_q = SCALE * (dot_wide(gn_ref[...], value_state, 1, 1) + grad_den * ks.whole[...]) * sq_ref[...]
    qs.src[pl.ds(0, 128)] = dot_exact_left(feat_ref[...], sk_ref[...], 0, 0)
    qs.src[pl.ds(128, 128)] = dot_exact_left(feat_ref[...], grad_q, 0, 0)
    in_ref[...] = dot_exact_right(grad_q, wq_ref[...], 1, 1)
    scatter(plane, qs.src, qs.got, QS1)

    gs.last[...] = take(gs.got2, GS2)
    gather(column, gs.last, gs.whole, GS3)

    gk.mid[...] = take(gk.got, GK1)[0:1]
    top = jnp.maximum(jnp.max(gk.got[...], axis=0)[1:2], 1e-30)
    to_code = 1.0 / top
    from_code = top * (1.0 / (32767.0 * 32767.0))
    wait(others_of(r_near), recv_sem.at[RA])

    for g in range(8):
        block = r_near[:, g].reshape(256, 256)
        terms = dot(to_natural, block)
        terms = terms[:, :128] + terms[:, 128:]
        code = jnp.minimum(jnp.sqrt(jnp.abs(terms) * to_code) * 32767.0 + 0.5, 32767.0)
        code = jnp.where(terms < 0, -code, code).astype(jnp.int32).astype(jnp.int16)
        r_far[pl.ds(g * 8, 8)] = code.reshape(8, 32, 128)
    give(far, lambda i: r_far.at[i], r_got, RB, 1, 3)
    r_got[far.me] = r_far[far.me]
    share(plane, gk.mid, gk.got2, GK2)

    wait(all_rows(gs.whole, column), recv_sem.at[GS3])
    grad_state = gs.whole[...]
    grad_k = dot_wide(v_ref[...], grad_state, 1, 1) * sk_ref[...]
    vg_ref[...] = grad_k
    pv.src[pl.ds(0, 128)] = dot_exact_left(feat_ref[...], grad_k, 0, 0)
    grad_v = gn_ref[...] + dot_wide(mk_ref[...], grad_state)
    pv.src[pl.ds(128, 128)] = dot_exact_left(feat_ref[...], grad_v, 0, 0)
    scatter(plane, pv.src, pv.got, PV1)
    in_ref[...] += dot_exact_right(grad_v, wv_ref[...], 1, 1)

    wait(others_of(f_far), recv_sem.at[FB])
    live = jnp.where(column_rows[...] >= 0, 1.0, 0.0)
    total = jnp.zeros((128, 128), F32)
    for r in range(4):
        rows = jnp.zeros((128, 128), F32)
        for n in range(4):
            term = dot(vals_ref[0, r, n], ext[col_ref[0, r, n]])
            rows = rows + term * live[r * 4 + n : r * 4 + n + 1]
        total = total + dot_exact_right(rows, cot_ref[pl.ds(r * 128, 128)], 0, 0)
    gg.src[...] = total
    scatter(column, gg.src, gg.got, GG1)
    give(far, lambda i: r_far.at[i], r_got, RB, 2, 3)
    qs.mid[...] = take(qs.got, QS1)
    share(column, qs.mid, qs.got2, QS2)

    pv.mid[...] = take(pv.got, PV1)
    share(column, pv.mid, pv.got2, PV2)
    gg.mid[...] = take(gg.got, GG1)
    share(plane, gg.mid, gg.got2, GG2)
    give(far, lambda i: r_far.at[i], r_got, RB, 3, 3)

    grad_ksum = take(gk.got2, GK2)
    gk.whole[...] = grad_ksum
    in_ref[...] += dot_exact_right(vg_ref[...] + grad_ksum * sk_ref[...], wk_ref[...], 1, 1)
    slopes = take(qs.got2, QS2)
    qs.last[...] = slopes
    chunk = take(pv.got2, PV2)
    pv.last[...] = jnp.where(plane.me < 16, chunk + slopes * gk.whole[...], chunk)
    gather(plane, pv.last, pv.whole, PV3)
    gather(plane, qs.last, qs.whole, QS3)

    gg.last[...] = take(gg.got2, GG2)
    gather(column, gg.last, gg.whole, GG3)

    wait(others_of(r_got), recv_sem.at[RB])

    to_slots = jnp.where(second == slot_row(first), 1.0, 0.0).astype(BF16)
    for g in range(8):
        code = r_got[pl.ds(g * 8, 8)].reshape(256, 128).astype(jnp.int32).astype(F32)
        block = jnp.concatenate(split(code * jnp.abs(code) * from_code), axis=1)
        r_rows[:, g] = dot(to_slots, block).astype(BF16).reshape(4, 64, 256)
    sums = jnp.zeros((512, 256), F32)
    for s in range(4):
        sums = sums + dot(onehot[s], r_rows[s].reshape(512, 256))
    returned = sums[:, :128] + sums[:, 128:]
    out_ref[...] = (in_ref[...] + own[...].reshape(512, 128) + returned).astype(BF16)

    wait(all_rows(qs.whole, plane), recv_sem.at[QS3])
    sums_ref[0] = qs.whole[pl.ds(128, 128)] * (1.0 / NODES)
    wait(all_rows(pv.whole, plane), recv_sem.at[PV3])
    sums_ref[1] = pv.whole[pl.ds(0, 128)] * (1.0 / NODES)
    sums_ref[2] = pv.whole[pl.ds(128, 128)] * (1.0 / NODES)
    wait(all_rows(gg.whole, column), recv_sem.at[GG3])
    sums_ref[3] = gg.whole[...] * (1.0 / NODES)
    for span, which in pending:
        wait(span, send_sem.at[which])


def shards(
    features, cotangent, w_query, w_key, w_value, w_graph, send_rows, block_col, block_count, block_vals
):
    vmem = pl.BlockSpec(memory_space=pltpu.VMEM)
    smem = pl.BlockSpec(memory_space=pltpu.SMEM)
    anywhere = pl.BlockSpec(memory_space=pltpu.HBM)
    wide = pltpu.VMEM((512, 128), F32)
    scratch = (
        [wide] * 9
        + row_buffers(1, 2)
        + row_buffers(2, 1)
        + sum_buffers(128, 16, 32)
        + sum_buffers(128, 16, 32)
        + sum_buffers(128, 16, 32)
        + sum_buffers(256, 32, 16)
        + sum_buffers(256, 32, 16)
        + [
            pltpu.VMEM((4, 512, 512), BF16),
            pltpu.VMEM((4, 64, 8, 128), F32),
            pltpu.VMEM((8, 8, 32, 128), BF16),
            pltpu.VMEM((8, 8, 32, 128), BF16),
            pltpu.VMEM((64, 32, 128), BF16),
            pltpu.VMEM((20, 128, 128), BF16),
            pltpu.VMEM((16, 128), jnp.int32),
            pltpu.VMEM((16, 128, 128), F32),
            pltpu.VMEM((4, 128, 128), F32),
            pltpu.VMEM((16, 128, 256), BF16),
            pltpu.VMEM((8, 8, 32, 256), BF16),
            pltpu.VMEM((8, 8, 32, 256), BF16),
            pltpu.VMEM((64, 32, 128), jnp.int16),
            pltpu.VMEM((64, 32, 128), jnp.int16),
            pltpu.VMEM((4, 8, 64, 256), BF16),
            pltpu.SemaphoreType.DMA((EXCHANGES,)),
            pltpu.SemaphoreType.DMA((EXCHANGES,)),
            pltpu.VMEM((512, 8), jnp.int32),
            pltpu.VMEM((512, 8), jnp.int32),
            pltpu.VMEM((512, 128), BF16),
            pltpu.VMEM((128, 128), BF16),
            pltpu.VMEM((128, 128), BF16),
            pltpu.VMEM((1, 4, 512), jnp.int32),
            pltpu.VMEM((512, 128), BF16),
            pltpu.VMEM((128, 128), BF16),
            pltpu.VMEM((1, 4, 4, 128, 128), BF16),
            pltpu.VMEM((128, 128), BF16),
            pltpu.SemaphoreType.DMA((8,)),
        ]
    )
    grad_features, sums = pl.pallas_call(
        layer_kernel,
        out_shape=(
            jax.ShapeDtypeStruct((512, 128), BF16),
            jax.ShapeDtypeStruct((4, 128, 128), F32),
        ),
        in_specs=[anywhere] * 8 + [smem, vmem, vmem],
        out_specs=(vmem, vmem),
        scratch_shapes=scratch,
        compiler_params=pltpu.CompilerParams(
            collective_id=0, has_side_effects=True, vmem_limit_bytes=60 << 20
        ),
        name="layer",
    )(
        features, cotangent, w_query, w_key, w_value, w_graph, jnp.swapaxes(send_rows, 1, 2), block_vals,
        block_col, block_col, block_count,
    )
    return grad_features, sums[0], sums[1], sums[2], sums[3]


def solution(mesh):
    both = ("dom", "sub")
    return jax.shard_map(
        shards,
        mesh=mesh,
        in_specs=(
            P(both, None), P(both, None), P(), P(), P(), P(),
            P(both, None, None), P(both, None, None), P(both, None), P(both, None, None, None, None),
        ),
        out_specs=(P(both, None), P(), P(), P(), P()),
        check_vma=False,
    )
```
